512 devices in a mesh: gx: 16 (over z_lo, y), gy: 32 (over x, z_hi, core).
Axes of the slice: x: 4, y: 4, z: 16 (z_hi: 4, z_lo: 4; z = z_hi * 4 + z_lo), core: 2. Of those that a mesh axis runs over, the one named last changes fastest.
Arguments:
- a_blocks: bfloat16 [64, 64, 5, 192, 192], P('gx', 'gy'), may hold values from -0.4375 to 0.4375
- a_codes: int32 [64, 64, 5], P('gx', 'gy'), may hold values from 0 to 9, as said below
- p_blocks: bfloat16 [64, 64, 3, 12, 192], P('gx', 'gy'), may hold values from -0.875 to 0.875
- p_codes: int32 [64, 64, 3], P('gx', 'gy'), may hold values from 0 to 5, as said below
Outputs:
- coarse: float32 [64, 64, 12, 588], P('gx', 'gy')
The draws below stay inside these ranges and needn't reach their ends.
Inputs may be any that keep to these rules, and one draw needn't show every extreme that they name: `a_codes`: slot 0 is 4 (the aggregate itself); the other slots of one aggregate hold distinct codes or 9; some aggregates have every slot live. `p_codes`: slot 0 is 0 (the aggregate itself); the other slots of one aggregate hold distinct codes of 1 to 4 or 5; some aggregates have every slot live.
All inputs are finite; a program needn't handle non-finite values.
Results may differ from the reference program's by a relative error of at most 0.0029.
Values may be sent and summed in bfloat16 or wider, within the bound.
A program may use at most 64 MiB of HBM per device.

```python
import jax
import jax.numpy as jnp
import numpy as np
from jax import lax

F = 192
C = 12
KA = 5
KP = 3
AGX = 64
AGY = 64


def draw_a_codes(key, part):
    first_key, second_key = jax.random.split(jax.random.fold_in(key, 11))
    scores = jax.random.randint(first_key, (AGX, AGY, 8), 0, 1 << 20) * 8 + jnp.arange(8, dtype=jnp.int32)
    order = jnp.argsort(scores, axis=-1).astype(jnp.int32)
    neighbours = jnp.where(order >= 4, order + 1, order)[..., :KA - 1]
    keep = jax.random.randint(second_key, (AGX, AGY, KA - 1), 0, 4) > 0
    row_x = jnp.arange(AGX, dtype=jnp.int32)[:, None]
    row_y = jnp.arange(AGY, dtype=jnp.int32)[None, :]
    filled = ((row_x + row_y) % 3 == 0)[..., None]
    neighbours = jnp.where(keep | filled, neighbours, 9)
    itself = jnp.full((AGX, AGY, 1), 4, jnp.int32)
    return jnp.concatenate([itself, neighbours], axis=-1).astype(jnp.int32)


def draw_p_codes(key, part):
    first_key, second_key = jax.random.split(jax.random.fold_in(key, 23))
    scores = jax.random.randint(first_key, (AGX, AGY, 4), 0, 1 << 20) * 4 + jnp.arange(4, dtype=jnp.int32)
    order = jnp.argsort(scores, axis=-1).astype(jnp.int32)
    neighbours = (order + 1)[..., :KP - 1]
    keep = jax.random.randint(second_key, (AGX, AGY, KP - 1), 0, 4) > 0
    row_x = jnp.arange(AGX, dtype=jnp.int32)[:, None]
    row_y = jnp.arange(AGY, dtype=jnp.int32)[None, :]
    filled = ((row_x + 2 * row_y) % 3 == 0)[..., None]
    neighbours = jnp.where(keep | filled, neighbours, 5)
    itself = jnp.zeros((AGX, AGY, 1), jnp.int32)
    return jnp.concatenate([itself, neighbours], axis=-1).astype(jnp.int32)


def block_scale(own_key, shape, cuts, least, high):
    gain, own = 1.0, jax.random.fold_in(own_key, 6)
    for axis_at, blocks in cuts:
        steps = jnp.exp(jax.random.uniform(jax.random.fold_in(own, axis_at), (blocks,), jnp.float32, least / len(cuts), high / len(cuts)))
        gain = gain * jnp.repeat(steps, shape[axis_at] // blocks).reshape([-1 if axis == axis_at else 1 for axis in range(len(shape))])
    return gain


def noise(key, dims, width, most, cuts=(), kind=jnp.bfloat16):
    result = width * jax.random.normal(key, dims, jnp.float32)
    if cuts:
        result = result * block_scale(key, dims, cuts, -0.22, 0.18)
    return jnp.clip(result, -most, most).astype(kind)


def setup_inputs(seed: int = 0) -> dict:
    key_list = jax.random.split(jax.random.key(seed), 5)
    a_blocks = noise(key_list[0], (AGX, AGY, KA, F, F), F ** -0.5, 0.4375, ((0, 16), (1, 32)))
    a_codes = draw_a_codes(jax.random.fold_in(key_list[4], 71), 0)
    p_blocks = noise(key_list[2], (AGX, AGY, KP, C, F), (F // 4) ** -0.5, 0.875, ((0, 16), (1, 32)))
    p_codes = draw_p_codes(jax.random.fold_in(key_list[4], 71), 0)
    return {"a_blocks": a_blocks, "a_codes": a_codes, "p_blocks": p_blocks, "p_codes": p_codes}


near_steps = tuple((shift_x, shift_y) for shift_x in (-1, 0, 1) for shift_y in (-1, 0, 1))
face_steps = ((0, 0), (-1, 0), (1, 0), (0, -1), (0, 1))


def spread_table():
    table = np.zeros((9, 5, 25), np.float32)
    for near_index, (shift_x, shift_y) in enumerate(near_steps):
        for face_index, (face_x, face_y) in enumerate(face_steps):
            table[near_index, face_index, (shift_x + face_x + 2) * 5 + shift_y + face_y + 2] = 1.0
    return table


def row_products(a_rows, a_slots, near_blocks):
    amount = a_rows.shape[0]
    flat_near = near_blocks.reshape((9 * amount,) + near_blocks.shape[2:])
    spread = jnp.asarray(spread_table()).reshape(9, 125)
    summed = jnp.zeros((amount, 25) + near_blocks.shape[3:], jnp.float32)
    for slot_index in range(a_slots.shape[1]):
        slot_codes = a_slots[:, slot_index]
        picked = (jnp.minimum(slot_codes, 8) * amount + jnp.arange(amount, dtype=jnp.int32)).astype(jnp.int32)
        chosen = flat_near[picked]
        product = jnp.einsum("nqcj,nij->nqci", chosen.astype(jnp.float32), a_rows[:, slot_index].astype(jnp.float32),
                             precision=lax.Precision.HIGHEST)
        weights = jnp.dot(jax.nn.one_hot(slot_codes, 9, dtype=jnp.float32), spread,
                          precision=lax.Precision.HIGHEST).reshape(amount, 5, 25)
        summed = summed + jnp.einsum("nqo,nqci->noci", weights, product, precision=lax.Precision.HIGHEST)
    return summed.astype(jnp.bfloat16)


def coarse_part(face_rows, coupled, face_index):
    terms = jnp.einsum("nci,noei->ncoe", face_rows.astype(jnp.float32), coupled.astype(jnp.float32),
                       precision=lax.Precision.HIGHEST)
    amount, unknowns = terms.shape[0], terms.shape[1]
    face_x, face_y = face_steps[face_index]
    layout = terms.reshape(amount, unknowns, 5, 5, unknowns)
    layout = jnp.pad(layout, ((0, 0), (0, 0), (1 - face_x, 1 + face_x), (1 - face_y, 1 + face_y), (0, 0)))
    return layout.reshape(amount, unknowns, 49 * unknowns)


def reference(a_blocks, a_codes, p_blocks, p_codes):
    face_blocks = jnp.einsum("xymf,xymcj->xyfcj", jax.nn.one_hot(p_codes, 5, dtype=jnp.float32),
                             p_blocks.astype(jnp.float32), precision=lax.Precision.HIGHEST).astype(jnp.bfloat16)
    widths = ((1, 1), (1, 1), (0, 0), (0, 0), (0, 0))
    padded_faces = jnp.pad(face_blocks, widths)
    columns = face_blocks.shape[1]

    def first(row_index):
        window = lax.dynamic_slice_in_dim(padded_faces, row_index, 3, 0)
        near_blocks = jnp.stack([window[1 + shift_x, 1 + shift_y:1 + shift_y + columns] for shift_x, shift_y in near_steps])
        return row_products(a_blocks[row_index], a_codes[row_index], near_blocks)

    row_ids = jnp.arange(face_blocks.shape[0], dtype=jnp.int32)
    coupled = lax.map(first, row_ids)
    padded_coupled = jnp.pad(coupled, widths)

    def second(row_index):
        face_window = lax.dynamic_slice_in_dim(padded_faces, row_index, 3, 0)
        coupled_window = lax.dynamic_slice_in_dim(padded_coupled, row_index, 3, 0)
        summed = jnp.zeros((columns, C, 49 * C), jnp.float32)
        for face_index, (face_x, face_y) in enumerate(face_steps):
            face_rows = face_window[1 - face_x, 1 - face_y:1 - face_y + columns, face_index]
            coupled_rows = coupled_window[1 - face_x, 1 - face_y:1 - face_y + columns]
            summed = summed + coarse_part(face_rows, coupled_rows, face_index)
        return summed

    return lax.map(second, row_ids)
```

```python
import functools

import jax
import jax.numpy as jnp
from jax import lax
from jax.experimental import pallas as pl
from jax.experimental.pallas import tpu as pltpu
from jax.sharding import PartitionSpec as P

WAYS = ((-1, 0), (1, 0), (0, -1), (0, 1), (-1, -1), (-1, 1), (1, -1), (1, 1))
FACES = ((0, 0), (-1, 0), (1, 0), (0, -1), (0, 1))
SLOT = 16
WIDE = 256
COLS = 384


def spread_out(piece, face, unknowns):
    face_x, face_y = face
    lane = lax.broadcasted_iota(jnp.int32, (piece.shape[0], 128), 1)
    tiles = [None] * 5
    for step in range(5):
        source = 5 * unknowns * step
        target = 7 * unknowns * (step + 1 - face_x) + unknowns * (1 - face_y)
        width = 5 * unknowns
        for i in range(source // 128, (source + width - 1) // 128 + 1):
            turned = piece[:, 128 * i : 128 * (i + 1)]
            turn = (target - source) % 128
            if turn:
                turned = pltpu.roll(turned, turn, 1)
            first = max(source, 128 * i) - source + target
            last = min(source + width, 128 * (i + 1)) - source + target
            for j in range(first // 128, (last - 1) // 128 + 1):
                low, high = max(first - 128 * j, 0), min(last - 128 * j, 128)
                part = jnp.where((lane >= low) & (lane < high), turned, 0.0)
                tiles[j] = part if tiles[j] is None else tiles[j] + part
    zero = jnp.zeros((piece.shape[0], 128), jnp.float32)
    return [zero if tile is None else tile for tile in tiles]


def kernel(
    a_ref, a_codes, p_ref, p_codes, out_ref,
    a_buf, p_buf, near, rows_w, own, to_send, received,
    a_sem, p_sem, send_near, recv_near, send_face, recv_face,
):
    tile_x, tile_y, slots_a, edges, _ = a_ref.shape
    slots_p, unknowns = p_ref.shape[2], p_ref.shape[3]
    span = slots_p * SLOT
    at_x, at_y = lax.axis_index("gx"), lax.axis_index("gy")
    count_x, count_y = lax.axis_size("gx"), lax.axis_size("gy")

    def inside(step_x, step_y):
        there_x, there_y = at_x + step_x, at_y + step_y
        return (there_x >= 0) & (there_x < count_x) & (there_y >= 0) & (there_y < count_y)

    p_copy = pltpu.make_async_copy(p_ref, p_buf, p_sem)
    p_copy.start()
    barrier = pltpu.get_barrier_semaphore()
    neighbours = jnp.int32(0)
    for step_x, step_y in WAYS:
        there = inside(step_x, step_y)
        neighbours += there.astype(jnp.int32)

        @pl.when(there)
        def _():
            pl.semaphore_signal(
                barrier, inc=1, device_id=(at_x + step_x, at_y + step_y), device_id_type=pl.DeviceIdType.MESH
            )

    a_copies = []
    for x in range(tile_x):
        for y in range(tile_y):
            copy = pltpu.make_async_copy(a_ref.at[x, y], a_buf.at[x * tile_y + y], a_sem.at[x * tile_y + y])
            copy.start()
            a_copies.append(copy)

    for step_x, step_y in WAYS:
        @pl.when(jnp.logical_not(inside(step_x, step_y)))
        def _():
            rows = {0: slice(1, tile_y + 1), -1: slice(0, 1), 1: slice(tile_y + 1, tile_y + 2)}[step_y]
            cols = {0: slice(1, tile_x + 1), -1: slice(0, 1), 1: slice(tile_x + 1, tile_x + 2)}[step_x]
            near[rows, cols] = jnp.zeros_like(near[rows, cols])

    for way in range(4):
        step_x, step_y = WAYS[way]

        @pl.when(jnp.logical_not(inside(-step_x, -step_y)))
        def _():
            received[way] = jnp.zeros(received.shape[1:], received.dtype)

    rows_w[:, :, edges:] = jnp.zeros((rows_w.shape[0], 2 * span, WIDE - edges), jnp.bfloat16)
    near[1 : tile_y + 1, 1 : tile_x + 1] = jnp.zeros((tile_y, tile_x, span, WIDE), jnp.bfloat16)

    p_copy.wait()
    row = lax.broadcasted_iota(jnp.int32, (span, WIDE - edges), 0)
    for x in range(tile_x):
        for y in range(tile_y):
            place = row % SLOT
            for m in range(slots_p):
                code = p_codes[x, y, m]
                block = p_buf[x, y, m]
                near[y + 1, x + 1, SLOT * m : SLOT * m + unknowns, :edges] = jnp.where(
                    code < 5, block, jnp.zeros_like(block)
                )
                shift = jnp.where(code == 1, -5, jnp.where(code == 2, 5, jnp.where(code == 3, -1, jnp.where(code == 4, 1, 0))))
                place = place + jnp.where(row // SLOT == m, shift * unknowns, 0)
            near[y + 1, x + 1, :, edges:] = place.astype(jnp.float32).astype(jnp.bfloat16)

    pl.semaphore_wait(barrier, neighbours)

    def near_copy(way):
        step_x, step_y = WAYS[way]
        from_y = {0: pl.ds(1, tile_y), -1: pl.ds(1, 1), 1: pl.ds(tile_y, 1)}[step_y]
        from_x = {0: pl.ds(1, tile_x), -1: pl.ds(1, 1), 1: pl.ds(tile_x, 1)}[step_x]
        to_y = {0: pl.ds(1, tile_y), -1: pl.ds(tile_y + 1, 1), 1: pl.ds(0, 1)}[step_y]
        to_x = {0: pl.ds(1, tile_x), -1: pl.ds(tile_x + 1, 1), 1: pl.ds(0, 1)}[step_x]
        return pltpu.make_async_remote_copy(
            src_ref=near.at[from_y, from_x],
            dst_ref=near.at[to_y, to_x],
            send_sem=send_near.at[way],
            recv_sem=recv_near.at[way],
            device_id=(at_x + step_x, at_y + step_y),
            device_id_type=pl.DeviceIdType.MESH,
        )

    def face_copy(way):
        step_x, step_y = WAYS[way]
        length = tile_x if step_x == 0 else tile_y
        return pltpu.make_async_remote_copy(
            src_ref=to_send.at[way, pl.ds(0, length)],
            dst_ref=received.at[way, pl.ds(0, length)],
            send_sem=send_face.at[way],
            recv_sem=recv_face.at[way],
            device_id=(at_x + step_x, at_y + step_y),
            device_id_type=pl.DeviceIdType.MESH,
        )

    def each_way(ways, make, does, sign):
        for way in ways:
            @pl.when(inside(sign * WAYS[way][0], sign * WAYS[way][1]))
            def _():
                does(make(way))

    each_way((3, 2, 5, 7, 4, 6, 1, 0), near_copy, lambda copy: copy.start(), 1)

    def first(f, _):
        pltpu.make_async_copy(a_ref.at[0, 0], a_buf.at[f], a_sem.at[f]).wait()
        here = near[f % tile_y + 1, f // tile_y + 1, :, :edges]
        for k in range(slots_a):
            product = jnp.dot(here, a_buf[f, k], preferred_element_type=jnp.float32)
            high = product.astype(jnp.bfloat16)
            rows_w[f * slots_a + k, :span, :edges] = high
            rows_w[f * slots_a + k, span:, :edges] = (product - high.astype(jnp.float32)).astype(jnp.bfloat16)
        return 0

    lax.fori_loop(0, tile_x * tile_y, first, 0)

    each_way(range(8), near_copy, lambda copy: copy.wait_recv(), -1)

    lane = lax.broadcasted_iota(jnp.int32, (span, COLS), 1).astype(jnp.float32)

    def second(f, _):
        x, y = f // tile_y, f % tile_y
        summed = jnp.zeros((span, COLS), jnp.float32)
        for k in range(slots_a):
            code = a_codes[x, y, k]
            live = code < 9
            code = jnp.where(live, code, 4)
            step_x, step_y = code // 3 - 1, code % 3 - 1
            there = near[y + 1 + step_y, x + 1 + step_x]
            base = jnp.where(live, unknowns * (5 * (step_x + 2) + step_y + 2), -4096).astype(jnp.float32)
            both = lax.dot_general(
                rows_w[f * slots_a + k], there, (((1,), (1,)), ((), ())), preferred_element_type=jnp.float32
            )
            block = (both[:span] + both[span:]).astype(jnp.bfloat16)
            target = there[:, edges : edges + 1].astype(jnp.float32) + base
            chosen = jnp.where(lane == target, 1.0, 0.0).astype(jnp.bfloat16)
            summed += jnp.dot(block, chosen, preferred_element_type=jnp.float32)
        own[0, f] = summed[:SLOT]
        for q in range(1, 5):
            value = jnp.zeros((SLOT, COLS), jnp.float32)
            for m in range(1, slots_p):
                value += jnp.where(p_codes[x, y, m] == q, summed[SLOT * m : SLOT * (m + 1)], 0.0)
            own[q, f] = value
        return 0

    lax.fori_loop(0, tile_x * tile_y, second, 0)

    for way in range(4):
        step_x, step_y = WAYS[way]
        edge_x = range(tile_x) if step_x == 0 else (tile_x - 1 if step_x > 0 else 0,)
        edge_y = range(tile_y) if step_y == 0 else (tile_y - 1 if step_y > 0 else 0,)
        for place, (x, y) in enumerate((x, y) for x in edge_x for y in edge_y):
            to_send[way, place] = own[way + 1, x * tile_y + y].astype(jnp.bfloat16)
    each_way((3, 2, 1, 0), face_copy, lambda copy: copy.start(), 1)
    each_way(range(4), face_copy, lambda copy: copy.wait_recv(), -1)

    for x in range(tile_x):
        for y in range(tile_y):
            total = None
            for q, (face_x, face_y) in enumerate(FACES):
                from_x, from_y = x - face_x, y - face_y
                if 0 <= from_x < tile_x and 0 <= from_y < tile_y:
                    piece = own[q, from_x * tile_y + from_y]
                else:
                    piece = received[q - 1, x if face_x == 0 else y].astype(jnp.float32)
                tiles = spread_out(piece, (face_x, face_y), unknowns)
                total = tiles if total is None else [s + t for s, t in zip(total, tiles)]
            for j, tile in enumerate(total):
                high = min(128 * (j + 1), out_ref.shape[3])
                out_ref[x, y, :, 128 * j : high] = tile[:unknowns, : high - 128 * j]

    each_way(range(8), near_copy, lambda copy: copy.wait_send(), 1)
    each_way(range(4), face_copy, lambda copy: copy.wait_send(), 1)


def shards(a_blocks, a_codes, p_blocks, p_codes):
    tile_x, tile_y, slots_a = a_codes.shape
    amount = tile_x * tile_y
    slots_p, unknowns, edges = p_blocks.shape[2:]
    span = slots_p * SLOT
    longest = max(tile_x, tile_y)
    dma = pltpu.SemaphoreType.DMA
    return pl.pallas_call(
        kernel,
        out_shape=jax.ShapeDtypeStruct((tile_x, tile_y, unknowns, 49 * unknowns), jnp.float32),
        in_specs=[
            pl.BlockSpec(memory_space=pl.ANY),
            pl.BlockSpec(memory_space=pltpu.SMEM),
            pl.BlockSpec(memory_space=pl.ANY),
            pl.BlockSpec(memory_space=pltpu.SMEM),
        ],
        out_specs=pl.BlockSpec(memory_space=pltpu.VMEM),
        scratch_shapes=[
            pltpu.VMEM((amount, slots_a, edges, edges), jnp.bfloat16),
            pltpu.VMEM(p_blocks.shape, jnp.bfloat16),
            pltpu.VMEM((tile_y + 2, tile_x + 2, span, WIDE), jnp.bfloat16),
            pltpu.VMEM((amount * slots_a, 2 * span, WIDE), jnp.bfloat16),
            pltpu.VMEM((5, amount, SLOT, COLS), jnp.float32),
            pltpu.VMEM((4, longest, SLOT, COLS), jnp.bfloat16),
            pltpu.VMEM((4, longest, SLOT, COLS), jnp.bfloat16),
            dma((amount,)),
            dma,
            dma((8,)),
            dma((8,)),
            dma((4,)),
            dma((4,)),
        ],
        compiler_params=pltpu.CompilerParams(
            collective_id=0, has_side_effects=True, vmem_limit_bytes=32 * 2**20
        ),
    )(a_blocks, a_codes, p_blocks, p_codes)


def solution(mesh):
    in_specs = (
        P("gx", "gy", None, None, None),
        P("gx", "gy", None),
        P("gx", "gy", None, None, None),
        P("gx", "gy", None),
    )
    out_specs = P("gx", "gy", None, None)
    return jax.shard_map(shards, mesh=mesh, in_specs=in_specs, out_specs=out_specs, check_vma=False)
```

```python
import functools

import jax
import jax.numpy as jnp
from jax import lax
from jax.experimental import pallas as pl
from jax.experimental.pallas import tpu as pltpu
from jax.sharding import PartitionSpec as P

WAYS = ((-1, 0), (1, 0), (0, -1), (0, 1), (-1, -1), (-1, 1), (1, -1), (1, 1))
FACES = ((0, 0), (-1, 0), (1, 0), (0, -1), (0, 1))
SLOT = 16
WIDE = 256
COLS = 384


def spread_out(piece, face, unknowns):
    face_x, face_y = face
    lane = lax.broadcasted_iota(jnp.int32, (piece.shape[0], 128), 1)
    tiles = [None] * 5
    for step in range(5):
        source = 5 * unknowns * step
        target = 7 * unknowns * (step + 1 - face_x) + unknowns * (1 - face_y)
        width = 5 * unknowns
        for i in range(source // 128, (source + width - 1) // 128 + 1):
            turned = piece[:, 128 * i : 128 * (i + 1)]
            turn = (target - source) % 128
            if turn:
                turned = pltpu.roll(turned, turn, 1)
            first = max(source, 128 * i) - source + target
            last = min(source + width, 128 * (i + 1)) - source + target
            for j in range(first // 128, (last - 1) // 128 + 1):
                low, high = max(first - 128 * j, 0), min(last - 128 * j, 128)
                part = jnp.where((lane >= low) & (lane < high), turned, 0.0)
                tiles[j] = part if tiles[j] is None else tiles[j] + part
    zero = jnp.zeros((piece.shape[0], 128), jnp.float32)
    return [zero if tile is None else tile for tile in tiles]


def kernel(
    a_ref, a_codes, p_ref, p_codes, out_ref,
    a_buf, p_buf, mid, inner_side, outer_side, rows_w, own, send_y, got_y, send_x, got_x,
    a_sem, p_sem, side_out, side_in, mid_out, mid_in, y_out, y_in, x_out, x_in,
):
    tile_x, tile_y, slots_a, edges, _ = a_ref.shape
    slots_p, unknowns = p_ref.shape[1], p_ref.shape[2]
    span = slots_p * SLOT
    at_x, at_y = lax.axis_index("gx"), lax.axis_index("gy")
    count_x, count_y = lax.axis_size("gx"), lax.axis_size("gy")
    outer = at_y % 2
    inner = 1 - outer
    rows = (inner, outer)
    sides = (inner_side, outer_side)

    def inside(step_x, step_y):
        there_x, there_y = at_x + step_x, at_y + step_y
        return (there_x >= 0) & (there_x < count_x) & (there_y >= 0) & (there_y < count_y)

    p_copy = pltpu.make_async_copy(p_ref, p_buf, p_sem)
    p_copy.start()
    barrier = pltpu.get_barrier_semaphore()
    neighbours = jnp.int32(0)
    for step_x, step_y in WAYS:
        there = inside(step_x, step_y)
        neighbours += there.astype(jnp.int32)

        @pl.when(there)
        def _():
            pl.semaphore_signal(
                barrier, inc=1, device_id=(at_x + step_x, at_y + step_y), device_id_type=pl.DeviceIdType.MESH
            )

    def a_copy(x, y):
        return pltpu.make_async_copy(a_ref.at[x, y], a_buf.at[x, y], a_sem.at[x, y])

    for y in (inner, outer):
        for x in range(tile_x):
            a_copy(x, y).start()

    for way in range(2):
        @pl.when(jnp.logical_not(inside(1 - 2 * way, 0)))
        def _():
            column = (tile_x + 1) * (1 - way)
            mid[:, column] = jnp.zeros((tile_y, span, WIDE), jnp.bfloat16)
            got_x[way] = jnp.zeros(got_x.shape[1:], got_x.dtype)

    for side in range(2):
        step_y = 2 * rows[side] - 1
        for step_x in (-1, 0, 1):
            @pl.when(jnp.logical_not(inside(step_x, step_y)))
            def _():
                columns = {0: slice(1, tile_x + 1), -1: slice(0, 1), 1: slice(tile_x + 1, tile_x + 2)}[step_x]
                sides[side][columns] = jnp.zeros_like(sides[side][columns])
                if step_x == 0:
                    got_y[side] = jnp.zeros(got_y.shape[1:], got_y.dtype)

    rows_w[:, :, :, :, edges:] = jnp.zeros((tile_x, tile_y, slots_a, 2 * span, WIDE - edges), jnp.bfloat16)

    p_copy.wait()
    taken = slots_p * unknowns * tile_y
    target_row = lax.broadcasted_iota(jnp.int32, (tile_y * span, taken), 0)
    source_row = lax.broadcasted_iota(jnp.int32, (tile_y * span, taken), 1)
    row = lax.broadcasted_iota(jnp.int32, (span, WIDE - edges), 0)
    for x in range(tile_x):
        wanted = jnp.full_like(target_row, -1)
        for y in range(tile_y):
            place = row % SLOT
            for m in range(slots_p):
                code = p_codes[m, y, x]
                first_row = y * span + m * SLOT
                fits = (target_row >= first_row) & (target_row < first_row + unknowns) & (code < 5)
                wanted = jnp.where(fits, (target_row - first_row + m * unknowns) * tile_y + y, wanted)
                shift = jnp.where(code == 1, -5, jnp.where(code == 2, 5, jnp.where(code == 3, -1, jnp.where(code == 4, 1, 0))))
                place = place + jnp.where(row // SLOT == m, shift * unknowns, 0)
            mid[y, x + 1, :, edges:] = place.astype(jnp.float32).astype(jnp.bfloat16)
        order = jnp.where(wanted == source_row, 1.0, 0.0).astype(jnp.bfloat16)
        laid = jnp.dot(order, p_buf[x].reshape(taken, edges), preferred_element_type=jnp.float32).astype(jnp.bfloat16)
        for y in range(tile_y):
            mid[y, x + 1, :, :edges] = laid[y * span : (y + 1) * span]

    def side_copy(step_x, side):
        source = {0: pl.ds(1, tile_x), -1: pl.ds(1, 1), 1: pl.ds(tile_x, 1)}[step_x]
        target = {0: pl.ds(1, tile_x), -1: pl.ds(tile_x + 1, 1), 1: pl.ds(0, 1)}[step_x]
        return pltpu.make_async_remote_copy(
            src_ref=mid.at[rows[side], source],
            dst_ref=sides[side].at[target],
            send_sem=side_out.at[side, step_x + 1],
            recv_sem=side_in.at[side, step_x + 1],
            device_id=(at_x + step_x, at_y + 2 * rows[side] - 1),
            device_id_type=pl.DeviceIdType.MESH,
        )

    def mid_copy(way):
        return pltpu.make_async_remote_copy(
            src_ref=mid.at[:, pl.ds(1 + (tile_x - 1) * way, 1)],
            dst_ref=mid.at[:, pl.ds((tile_x + 1) * (1 - way), 1)],
            send_sem=mid_out.at[way],
            recv_sem=mid_in.at[way],
            device_id=(at_x + 2 * way - 1, at_y),
            device_id_type=pl.DeviceIdType.MESH,
        )

    def y_copy(side):
        return pltpu.make_async_remote_copy(
            src_ref=send_y.at[side],
            dst_ref=got_y.at[side],
            send_sem=y_out.at[side],
            recv_sem=y_in.at[side],
            device_id=(at_x, at_y + 2 * rows[side] - 1),
            device_id_type=pl.DeviceIdType.MESH,
        )

    def x_copy(way, side):
        return pltpu.make_async_remote_copy(
            src_ref=send_x.at[way, side],
            dst_ref=got_x.at[way, side],
            send_sem=x_out.at[way, side],
            recv_sem=x_in.at[way, side],
            device_id=(at_x + 2 * way - 1, at_y),
            device_id_type=pl.DeviceIdType.MESH,
        )

    def when_inside(step_x, step_y, does):
        pl.when(inside(step_x, step_y))(does)

    def first(y):
        for x in range(tile_x):
            a_copy(x, y).wait()
            here = mid[y, x + 1, :, :edges]
            for k in range(slots_a):
                product = jnp.dot(here, a_buf[x, y, k], preferred_element_type=jnp.float32)
                high = product.astype(jnp.bfloat16)
                rows_w[x, y, k, :span, :edges] = high
                rows_w[x, y, k, span:, :edges] = (product - high.astype(jnp.float32)).astype(jnp.bfloat16)

    lane = lax.broadcasted_iota(jnp.int32, (span, COLS), 1).astype(jnp.float32)

    def second(side):
        y = rows[side]
        for x in range(tile_x):
            summed = jnp.zeros((span, COLS), jnp.float32)
            for k in range(slots_a):
                code = a_codes[x, y, k]
                live = code < 9
                code = jnp.where(live, code, 4)
                step_x, step_y = code // 3 - 1, code % 3 - 1
                there = jnp.where(
                    step_y == 2 * y - 1,
                    sides[side][x + 1 + step_x],
                    mid[jnp.clip(y + step_y, 0, tile_y - 1), x + 1 + step_x],
                )
                base = jnp.where(live, unknowns * (5 * (step_x + 2) + step_y + 2), -4096).astype(jnp.float32)
                both = lax.dot_general(
                    rows_w[x, y, k], there, (((1,), (1,)), ((), ())), preferred_element_type=jnp.float32
                )
                block = (both[:span] + both[span:]).astype(jnp.bfloat16)
                target = there[:, edges : edges + 1].astype(jnp.float32) + base
                chosen = jnp.where(lane == target, 1.0, 0.0).astype(jnp.bfloat16)
                summed += jnp.dot(block, chosen, preferred_element_type=jnp.float32)
            own[0, x, y] = summed[:SLOT]
            for q in range(1, 5):
                value = jnp.zeros((SLOT, COLS), jnp.float32)
                for m in range(1, slots_p):
                    value += jnp.where(p_codes[m, y, x] == q, summed[SLOT * m : SLOT * (m + 1)], 0.0)
                own[q, x, y] = value

    def send_contributions(side):
        y = rows[side]
        for x in range(tile_x):
            send_y[side, x] = own[y + 3, x, y].astype(jnp.bfloat16)
        when_inside(0, 2 * y - 1, lambda: y_copy(side).start())
        for way in range(2):
            send_x[way, side] = own[way + 1, (tile_x - 1) * way, y].astype(jnp.bfloat16)
            when_inside(2 * way - 1, 0, lambda: x_copy(way, side).start())

    pl.semaphore_wait(barrier, neighbours)
    for step_x in (0, -1, 1):
        when_inside(step_x, 2 * outer - 1, lambda: side_copy(step_x, 1).start())
    for way in range(2):
        when_inside(2 * way - 1, 0, lambda: mid_copy(way).start())
    for step_x in (0, -1, 1):
        when_inside(step_x, 2 * inner - 1, lambda: side_copy(step_x, 0).start())

    def both_firsts(i, _):
        first(jnp.where(i == 0, inner, outer))
        return 0

    lax.fori_loop(0, 2, both_firsts, 0)

    for way in range(2):
        when_inside(1 - 2 * way, 0, lambda: mid_copy(way).wait_recv())
    for side in range(2):
        for step_x in (0, -1, 1):
            when_inside(-step_x, 2 * rows[side] - 1, lambda: side_copy(step_x, side).wait_recv())
        second(side)
        send_contributions(side)

    def put(x, y, pieces, add):
        total = None
        for piece, face in pieces:
            tiles = spread_out(piece.astype(jnp.float32), FACES[face], unknowns)
            total = tiles if total is None else [s + t for s, t in zip(total, tiles)]
        for j, tile in enumerate(total):
            high = min(128 * (j + 1), out_ref.shape[3])
            tile = tile[:unknowns, : high - 128 * j]
            if add:
                tile = tile + out_ref[x, y, :, 128 * j : high]
            out_ref[x, y, :, 128 * j : high] = tile

    for x in range(tile_x):
        for y in range(tile_y):
            pieces = []
            for face, (face_x, face_y) in enumerate(FACES):
                from_x, from_y = x - face_x, y - face_y
                if 0 <= from_x < tile_x and 0 <= from_y < tile_y:
                    pieces.append((own[face, from_x, from_y], face))
            put(x, y, pieces, False)

    for way in range(2):
        for side in range(2):
            when_inside(1 - 2 * way, 0, lambda: x_copy(way, side).wait_recv())
    for side in range(2):
        when_inside(0, 2 * rows[side] - 1, lambda: y_copy(side).wait_recv())

    for x in range(tile_x):
        for y in range(tile_y):
            side = outer if y else inner
            pieces = [(got_y[side, x], 4 - y)]
            if x == 0:
                pieces.append((got_x[1, side], 2))
            if x == tile_x - 1:
                pieces.append((got_x[0, side], 1))
            put(x, y, pieces, True)

    for side in range(2):
        for step_x in (-1, 0, 1):
            when_inside(step_x, 2 * rows[side] - 1, lambda: side_copy(step_x, side).wait_send())
        when_inside(0, 2 * rows[side] - 1, lambda: y_copy(side).wait_send())
        for way in range(2):
            when_inside(2 * way - 1, 0, lambda: x_copy(way, side).wait_send())
    for way in range(2):
        when_inside(2 * way - 1, 0, lambda: mid_copy(way).wait_send())


def shards(a_blocks, a_codes, p_blocks, p_codes):
    tile_x, tile_y, slots_a = a_codes.shape
    slots_p, unknowns, edges = p_blocks.shape[2:]
    span = slots_p * SLOT
    dma = pltpu.SemaphoreType.DMA
    return pl.pallas_call(
        kernel,
        out_shape=jax.ShapeDtypeStruct((tile_x, tile_y, unknowns, 49 * unknowns), jnp.float32),
        in_specs=[
            pl.BlockSpec(memory_space=pltpu.HBM),
            pl.BlockSpec(memory_space=pltpu.SMEM),
            pl.BlockSpec(memory_space=pltpu.HBM),
            pl.BlockSpec(memory_space=pltpu.SMEM),
        ],
        out_specs=pl.BlockSpec(memory_space=pltpu.VMEM),
        scratch_shapes=[
            pltpu.VMEM((tile_x, tile_y, slots_a, edges, edges), jnp.bfloat16),
            pltpu.VMEM((tile_x, slots_p, unknowns, tile_y, edges), jnp.bfloat16),
            pltpu.VMEM((tile_y, tile_x + 2, span, WIDE), jnp.bfloat16),
            pltpu.VMEM((tile_x + 2, span, WIDE), jnp.bfloat16),
            pltpu.VMEM((tile_x + 2, span, WIDE), jnp.bfloat16),
            pltpu.VMEM((tile_x, tile_y, slots_a, 2 * span, WIDE), jnp.bfloat16),
            pltpu.VMEM((5, tile_x, tile_y, SLOT, COLS), jnp.float32),
            pltpu.VMEM((tile_y, tile_x, SLOT, COLS), jnp.bfloat16),
            pltpu.VMEM((tile_y, tile_x, SLOT, COLS), jnp.bfloat16),
            pltpu.VMEM((2, tile_y, SLOT, COLS), jnp.bfloat16),
            pltpu.VMEM((2, tile_y, SLOT, COLS), jnp.bfloat16),
            dma((tile_x, tile_y)),
            dma,
            dma((2, 3)),
            dma((2, 3)),
            dma((2,)),
            dma((2,)),
            dma((2,)),
            dma((2,)),
            dma((2, 2)),
            dma((2, 2)),
        ],
        compiler_params=pltpu.CompilerParams(
            collective_id=0, has_side_effects=True, vmem_limit_bytes=40 * 2**20
        ),
    )(pltpu.with_memory_space_constraint(a_blocks, pltpu.HBM), pltpu.with_memory_space_constraint(a_codes, pltpu.HBM), pltpu.with_memory_space_constraint(jnp.transpose(p_blocks, (0, 2, 3, 1, 4)), pltpu.HBM), pltpu.with_memory_space_constraint(jnp.transpose(p_codes, (2, 1, 0)), pltpu.HBM))


def solution(mesh):
    in_specs = (
        P("gx", "gy", None, None, None),
        P("gx", "gy", None),
        P("gx", "gy", None, None, None),
        P("gx", "gy", None),
    )
    out_specs = P("gx", "gy", None, None)
    return jax.shard_map(shards, mesh=mesh, in_specs=in_specs, out_specs=out_specs, check_vma=False)
```

```python
import functools

import jax
import jax.numpy as jnp
from jax import lax
from jax.experimental import pallas as pl
from jax.experimental.pallas import tpu as pltpu
from jax.sharding import PartitionSpec as P

WAYS = ((-1, 0), (1, 0), (0, -1), (0, 1), (-1, -1), (-1, 1), (1, -1), (1, 1))
FACES = ((0, 0), (-1, 0), (1, 0), (0, -1), (0, 1))
SLOT = 16
WIDE = 256
PACK = 64
COLS = 384


def spread_out(piece, face, unknowns):
    face_x, face_y = face
    lane = lax.broadcasted_iota(jnp.int32, (piece.shape[0], 128), 1)
    tiles = [None] * 5
    for step in range(5):
        source = 5 * unknowns * step
        target = 7 * unknowns * (step + 1 - face_x) + unknowns * (1 - face_y)
        width = 5 * unknowns
        for i in range(source // 128, (source + width - 1) // 128 + 1):
            turned = piece[:, 128 * i : 128 * (i + 1)]
            turn = (target - source) % 128
            if turn:
                turned = pltpu.roll(turned, turn, 1)
            first = max(source, 128 * i) - source + target
            last = min(source + width, 128 * (i + 1)) - source + target
            for j in range(first // 128, (last - 1) // 128 + 1):
                low, high = max(first - 128 * j, 0), min(last - 128 * j, 128)
                part = jnp.where((lane >= low) & (lane < high), turned, 0.0)
                tiles[j] = part if tiles[j] is None else tiles[j] + part
    zero = jnp.zeros((piece.shape[0], 128), jnp.float32)
    return [zero if tile is None else tile for tile in tiles]


def one_hot(wanted, source):
    return jnp.where(wanted == source, 1.0, 0.0).astype(jnp.bfloat16)


def pack(block, slots, unknowns):
    span, used = block.shape[0], slots * unknowns
    lane = lax.broadcasted_iota(jnp.int32, (span, 128), 1)
    rest = block[:, 128:].astype(jnp.float32)
    turned = pltpu.roll(rest, 64, 1)
    zero = jnp.zeros_like(rest)
    parts = [jnp.where(lane < 64, rest, zero), jnp.where(lane < 64, zero, turned), jnp.where(lane < 64, turned, rest)]
    stacked = jnp.concatenate([block[:, :128]] + [part.astype(jnp.bfloat16) for part in parts], axis=0)
    row = lax.broadcasted_iota(jnp.int32, (PACK, 4 * span), 0)
    source = lax.broadcasted_iota(jnp.int32, (PACK, 4 * span), 1)
    part, at = source // span, source % span
    dense = at // SLOT * unknowns + at % SLOT
    dense = jnp.where(at % SLOT < unknowns, dense, -1)
    half = used // 2
    low = jnp.where((dense >= 0) & (dense < half), used + dense, -1)
    high = jnp.where(dense >= half, used + dense - half, -1)
    mark = jnp.where(at % SLOT == 0, used + half + at // SLOT, -1)
    goes = jnp.where(part == 0, dense, jnp.where(part == 1, low, jnp.where(part == 2, high, mark)))
    return jnp.dot(one_hot(goes, row), stacked, preferred_element_type=jnp.float32).astype(jnp.bfloat16)


def unpack(packed, slots, unknowns):
    span, used = slots * SLOT, slots * unknowns
    row = lax.broadcasted_iota(jnp.int32, (3 * span, PACK), 0)
    source = lax.broadcasted_iota(jnp.int32, (3 * span, PACK), 1)
    part, at = row // span, row % span
    dense = at // SLOT * unknowns + at % SLOT
    half = used // 2
    folded = used + jnp.where(dense < half, dense, dense - half)
    comes = jnp.where(part == 0, dense, jnp.where(part == 1, folded, used + half + at // SLOT))
    comes = jnp.where((at % SLOT < unknowns) | (part == 2), comes, -1)
    laid = jnp.dot(one_hot(comes, source), packed, preferred_element_type=jnp.float32)
    lane = lax.broadcasted_iota(jnp.int32, (span, 128), 1)
    at = lax.broadcasted_iota(jnp.int32, (span, 128), 0)
    rest = laid[span : 2 * span]
    rest = jnp.where(at // SLOT * unknowns + at % SLOT < half, rest, pltpu.roll(rest, 64, 1))
    rest = jnp.where(lane < 64, rest, laid[2 * span :] + (at % SLOT).astype(jnp.float32))
    return laid[:span].astype(jnp.bfloat16), rest.astype(jnp.bfloat16)


def kernel(
    a_ref, a_codes, p_ref, p_codes, out_ref,
    a_buf, p_buf, mid, inner_side, outer_side, packed, got, rows_w, own, send_y, got_y, send_x, got_x,
    a_sem, p_sem, side_out, side_in, mid_out, mid_in, y_out, y_in, x_out, x_in,
):
    tile_x, tile_y, slots_a, edges, _ = a_ref.shape
    slots_p, unknowns = p_ref.shape[1], p_ref.shape[2]
    span = slots_p * SLOT
    at_x, at_y = lax.axis_index("gx"), lax.axis_index("gy")
    count_x, count_y = lax.axis_size("gx"), lax.axis_size("gy")
    outer = at_y % 2
    inner = 1 - outer
    rows = (inner, outer)
    sides = (inner_side, outer_side)

    def inside(step_x, step_y):
        there_x, there_y = at_x + step_x, at_y + step_y
        return (there_x >= 0) & (there_x < count_x) & (there_y >= 0) & (there_y < count_y)

    p_copy = pltpu.make_async_copy(p_ref, p_buf, p_sem)
    p_copy.start()
    barrier = pltpu.get_barrier_semaphore()
    neighbours = jnp.int32(0)
    for step_x, step_y in WAYS:
        there = inside(step_x, step_y)
        neighbours += there.astype(jnp.int32)

        @pl.when(there)
        def _():
            pl.semaphore_signal(
                barrier, inc=1, device_id=(at_x + step_x, at_y + step_y), device_id_type=pl.DeviceIdType.MESH
            )

    def a_copy(x, y):
        return pltpu.make_async_copy(a_ref.at[x, y], a_buf.at[x, y], a_sem.at[x, y])

    for y in (inner, outer):
        for x in range(tile_x):
            a_copy(x, y).start()

    for way in range(2):
        @pl.when(jnp.logical_not(inside(1 - 2 * way, 0)))
        def _():
            column = (tile_x + 1) * (1 - way)
            mid[:, column] = jnp.zeros((tile_y, span, WIDE), jnp.bfloat16)
            got_x[way] = jnp.zeros(got_x.shape[1:], got_x.dtype)

    for side in range(2):
        step_y = 2 * rows[side] - 1
        for step_x in (-1, 0, 1):
            @pl.when(jnp.logical_not(inside(step_x, step_y)))
            def _():
                columns = {0: slice(1, tile_x + 1), -1: slice(0, 1), 1: slice(tile_x + 1, tile_x + 2)}[step_x]
                holds = got if side else inner_side
                holds[columns] = jnp.zeros_like(holds[columns])
                if step_x == 0:
                    got_y[side] = jnp.zeros(got_y.shape[1:], got_y.dtype)

    rows_w[:, :, :, :, edges:] = jnp.zeros((tile_x, tile_y, slots_a, 2 * span, WIDE - edges), jnp.bfloat16)

    p_copy.wait()
    taken = slots_p * unknowns * tile_y
    target_row = lax.broadcasted_iota(jnp.int32, (tile_y * span, taken), 0)
    source_row = lax.broadcasted_iota(jnp.int32, (tile_y * span, taken), 1)
    row = lax.broadcasted_iota(jnp.int32, (span, WIDE - edges), 0)
    for x in range(tile_x):
        wanted = jnp.full_like(target_row, -1)
        for y in range(tile_y):
            place = row % SLOT
            for m in range(slots_p):
                code = p_codes[m, y, x]
                first_row = y * span + m * SLOT
                fits = (target_row >= first_row) & (target_row < first_row + unknowns) & (code < 5)
                wanted = jnp.where(fits, (target_row - first_row + m * unknowns) * tile_y + y, wanted)
                shift = jnp.where(code == 1, -5, jnp.where(code == 2, 5, jnp.where(code == 3, -1, jnp.where(code == 4, 1, 0))))
                place = place + jnp.where(row // SLOT == m, shift * unknowns, 0)
            mid[y, x + 1, :, edges:] = place.astype(jnp.float32).astype(jnp.bfloat16)
        order = jnp.where(wanted == source_row, 1.0, 0.0).astype(jnp.bfloat16)
        laid = jnp.dot(order, p_buf[x].reshape(taken, edges), preferred_element_type=jnp.float32).astype(jnp.bfloat16)
        for y in range(tile_y):
            mid[y, x + 1, :, :edges] = laid[y * span : (y + 1) * span]

    def side_copy(step_x, side):
        source = {0: pl.ds(1, tile_x), -1: pl.ds(1, 1), 1: pl.ds(tile_x, 1)}[step_x]
        target = {0: pl.ds(1, tile_x), -1: pl.ds(tile_x + 1, 1), 1: pl.ds(0, 1)}[step_x]
        return pltpu.make_async_remote_copy(
            src_ref=packed.at[pl.ds(source.start - 1, source.size)] if side else mid.at[inner, source],
            dst_ref=(got if side else inner_side).at[target],
            send_sem=side_out.at[side, step_x + 1],
            recv_sem=side_in.at[side, step_x + 1],
            device_id=(at_x + step_x, at_y + 2 * rows[side] - 1),
            device_id_type=pl.DeviceIdType.MESH,
        )

    def mid_copy(way):
        return pltpu.make_async_remote_copy(
            src_ref=mid.at[:, pl.ds(1 + (tile_x - 1) * way, 1)],
            dst_ref=mid.at[:, pl.ds((tile_x + 1) * (1 - way), 1)],
            send_sem=mid_out.at[way],
            recv_sem=mid_in.at[way],
            device_id=(at_x + 2 * way - 1, at_y),
            device_id_type=pl.DeviceIdType.MESH,
        )

    def y_copy(side):
        return pltpu.make_async_remote_copy(
            src_ref=send_y.at[side],
            dst_ref=got_y.at[side],
            send_sem=y_out.at[side],
            recv_sem=y_in.at[side],
            device_id=(at_x, at_y + 2 * rows[side] - 1),
            device_id_type=pl.DeviceIdType.MESH,
        )

    def x_copy(way, side):
        return pltpu.make_async_remote_copy(
            src_ref=send_x.at[way, side],
            dst_ref=got_x.at[way, side],
            send_sem=x_out.at[way, side],
            recv_sem=x_in.at[way, side],
            device_id=(at_x + 2 * way - 1, at_y),
            device_id_type=pl.DeviceIdType.MESH,
        )

    def when_inside(step_x, step_y, does):
        pl.when(inside(step_x, step_y))(does)

    def first(y):
        for x in range(tile_x):
            a_copy(x, y).wait()
            here = mid[y, x + 1, :, :edges]
            for k in range(slots_a):
                product = jnp.dot(here, a_buf[x, y, k], preferred_element_type=jnp.float32)
                high = product.astype(jnp.bfloat16)
                rows_w[x, y, k, :span, :edges] = high
                rows_w[x, y, k, span:, :edges] = (product - high.astype(jnp.float32)).astype(jnp.bfloat16)

    lane = lax.broadcasted_iota(jnp.int32, (span, COLS), 1).astype(jnp.float32)

    def second(side):
        y = rows[side]
        for x in range(tile_x):
            summed = jnp.zeros((span, COLS), jnp.float32)
            for k in range(slots_a):
                code = a_codes[x, y, k]
                live = code < 9
                code = jnp.where(live, code, 4)
                step_x, step_y = code // 3 - 1, code % 3 - 1
                there = jnp.where(
                    step_y == 2 * y - 1,
                    sides[side][x + 1 + step_x],
                    mid[jnp.clip(y + step_y, 0, tile_y - 1), x + 1 + step_x],
                )
                base = jnp.where(live, unknowns * (5 * (step_x + 2) + step_y + 2), -4096).astype(jnp.float32)
                both = lax.dot_general(
                    rows_w[x, y, k], there, (((1,), (1,)), ((), ())), preferred_element_type=jnp.float32
                )
                block = (both[:span] + both[span:]).astype(jnp.bfloat16)
                target = there[:, edges : edges + 1].astype(jnp.float32) + base
                chosen = jnp.where(lane == target, 1.0, 0.0).astype(jnp.bfloat16)
                summed += jnp.dot(block, chosen, preferred_element_type=jnp.float32)
            own[0, x, y] = summed[:SLOT]
            for q in range(1, 5):
                value = jnp.zeros((SLOT, COLS), jnp.float32)
                for m in range(1, slots_p):
                    value += jnp.where(p_codes[m, y, x] == q, summed[SLOT * m : SLOT * (m + 1)], 0.0)
                own[q, x, y] = value

    def send_contributions(side):
        y = rows[side]
        for x in range(tile_x):
            send_y[side, x] = own[y + 3, x, y].astype(jnp.bfloat16)
        when_inside(0, 2 * y - 1, lambda: y_copy(side).start())
        for way in range(2):
            send_x[way, side] = own[way + 1, (tile_x - 1) * way, y].astype(jnp.bfloat16)
            when_inside(2 * way - 1, 0, lambda: x_copy(way, side).start())

    for x in range(tile_x):
        packed[x] = pack(mid[outer, x + 1], slots_p, unknowns)

    pl.semaphore_wait(barrier, neighbours)
    for step_x in (0, -1, 1):
        when_inside(step_x, 2 * outer - 1, lambda: side_copy(step_x, 1).start())
    for way in range(2):
        when_inside(2 * way - 1, 0, lambda: mid_copy(way).start())
    for step_x in (0, -1, 1):
        when_inside(step_x, 2 * inner - 1, lambda: side_copy(step_x, 0).start())

    def both_firsts(i, _):
        first(jnp.where(i == 0, inner, outer))
        return 0

    lax.fori_loop(0, 2, both_firsts, 0)

    for way in range(2):
        when_inside(1 - 2 * way, 0, lambda: mid_copy(way).wait_recv())
    for side in range(2):
        for step_x in (0, -1, 1):
            when_inside(-step_x, 2 * rows[side] - 1, lambda: side_copy(step_x, side).wait_recv())
        if side:
            for x in range(tile_x + 2):
                outer_side[x, :, :128], outer_side[x, :, 128:] = unpack(got[x], slots_p, unknowns)
        second(side)
        send_contributions(side)

    def put(x, y, pieces, add):
        total = None
        for piece, face in pieces:
            tiles = spread_out(piece.astype(jnp.float32), FACES[face], unknowns)
            total = tiles if total is None else [s + t for s, t in zip(total, tiles)]
        for j, tile in enumerate(total):
            high = min(128 * (j + 1), out_ref.shape[3])
            tile = tile[:unknowns, : high - 128 * j]
            if add:
                tile = tile + out_ref[x, y, :, 128 * j : high]
            out_ref[x, y, :, 128 * j : high] = tile

    for x in range(tile_x):
        for y in range(tile_y):
            pieces = []
            for face, (face_x, face_y) in enumerate(FACES):
                from_x, from_y = x - face_x, y - face_y
                if 0 <= from_x < tile_x and 0 <= from_y < tile_y:
                    pieces.append((own[face, from_x, from_y], face))
            put(x, y, pieces, False)

    for way in range(2):
        for side in range(2):
            when_inside(1 - 2 * way, 0, lambda: x_copy(way, side).wait_recv())
    for side in range(2):
        when_inside(0, 2 * rows[side] - 1, lambda: y_copy(side).wait_recv())

    for x in range(tile_x):
        for y in range(tile_y):
            side = outer if y else inner
            pieces = [(got_y[side, x], 4 - y)]
            if x == 0:
                pieces.append((got_x[1, side], 2))
            if x == tile_x - 1:
                pieces.append((got_x[0, side], 1))
            put(x, y, pieces, True)

    for side in range(2):
        for step_x in (-1, 0, 1):
            when_inside(step_x, 2 * rows[side] - 1, lambda: side_copy(step_x, side).wait_send())
        when_inside(0, 2 * rows[side] - 1, lambda: y_copy(side).wait_send())
        for way in range(2):
            when_inside(2 * way - 1, 0, lambda: x_copy(way, side).wait_send())
    for way in range(2):
        when_inside(2 * way - 1, 0, lambda: mid_copy(way).wait_send())


def shards(a_blocks, a_codes, p_blocks, p_codes):
    tile_x, tile_y, slots_a = a_codes.shape
    slots_p, unknowns, edges = p_blocks.shape[2:]
    span = slots_p * SLOT
    dma = pltpu.SemaphoreType.DMA
    return pl.pallas_call(
        kernel,
        out_shape=jax.ShapeDtypeStruct((tile_x, tile_y, unknowns, 49 * unknowns), jnp.float32),
        in_specs=[
            pl.BlockSpec(memory_space=pltpu.HBM),
            pl.BlockSpec(memory_space=pltpu.SMEM),
            pl.BlockSpec(memory_space=pltpu.HBM),
            pl.BlockSpec(memory_space=pltpu.SMEM),
        ],
        out_specs=pl.BlockSpec(memory_space=pltpu.VMEM),
        scratch_shapes=[
            pltpu.VMEM((tile_x, tile_y, slots_a, edges, edges), jnp.bfloat16),
            pltpu.VMEM((tile_x, slots_p, unknowns, tile_y, edges), jnp.bfloat16),
            pltpu.VMEM((tile_y, tile_x + 2, span, WIDE), jnp.bfloat16),
            pltpu.VMEM((tile_x + 2, span, WIDE), jnp.bfloat16),
            pltpu.VMEM((tile_x + 2, span, WIDE), jnp.bfloat16),
            pltpu.VMEM((tile_x, PACK, 128), jnp.bfloat16),
            pltpu.VMEM((tile_x + 2, PACK, 128), jnp.bfloat16),
            pltpu.VMEM((tile_x, tile_y, slots_a, 2 * span, WIDE), jnp.bfloat16),
            pltpu.VMEM((5, tile_x, tile_y, SLOT, COLS), jnp.float32),
            pltpu.VMEM((tile_y, tile_x, SLOT, COLS), jnp.bfloat16),
            pltpu.VMEM((tile_y, tile_x, SLOT, COLS), jnp.bfloat16),
            pltpu.VMEM((2, tile_y, SLOT, COLS), jnp.bfloat16),
            pltpu.VMEM((2, tile_y, SLOT, COLS), jnp.bfloat16),
            dma((tile_x, tile_y)),
            dma,
            dma((2, 3)),
            dma((2, 3)),
            dma((2,)),
            dma((2,)),
            dma((2,)),
            dma((2,)),
            dma((2, 2)),
            dma((2, 2)),
        ],
        compiler_params=pltpu.CompilerParams(
            collective_id=0, has_side_effects=True, vmem_limit_bytes=40 * 2**20
        ),
    )(pltpu.with_memory_space_constraint(a_blocks, pltpu.HBM), pltpu.with_memory_space_constraint(a_codes, pltpu.HBM), pltpu.with_memory_space_constraint(jnp.transpose(p_blocks, (0, 2, 3, 1, 4)), pltpu.HBM), pltpu.with_memory_space_constraint(jnp.transpose(p_codes, (2, 1, 0)), pltpu.HBM))


def solution(mesh):
    in_specs = (
        P("gx", "gy", None, None, None),
        P("gx", "gy", None),
        P("gx", "gy", None, None, None),
        P("gx", "gy", None),
    )
    out_specs = P("gx", "gy", None, None)
    return jax.shard_map(shards, mesh=mesh, in_specs=in_specs, out_specs=out_specs, check_vma=False)
```

```python
import functools

import jax
import jax.numpy as jnp
from jax import lax
from jax.experimental import pallas as pl
from jax.experimental.pallas import tpu as pltpu
from jax.sharding import PartitionSpec as P

WAYS = ((-1, 0), (1, 0), (0, -1), (0, 1), (-1, -1), (-1, 1), (1, -1), (1, 1))
FACES = ((0, 0), (-1, 0), (1, 0), (0, -1), (0, 1))
SLOT = 16
WIDE = 256
PACK = 64
COLS = 384


def spread_out(piece, face, unknowns):
    face_x, face_y = face
    lane = lax.broadcasted_iota(jnp.int32, (piece.shape[0], 128), 1)
    tiles = [None] * 5
    for step in range(5):
        source = 5 * unknowns * step
        target = 7 * unknowns * (step + 1 - face_x) + unknowns * (1 - face_y)
        width = 5 * unknowns
        for i in range(source // 128, (source + width - 1) // 128 + 1):
            turned = piece[:, 128 * i : 128 * (i + 1)]
            turn = (target - source) % 128
            if turn:
                turned = pltpu.roll(turned, turn, 1)
            first = max(source, 128 * i) - source + target
            last = min(source + width, 128 * (i + 1)) - source + target
            for j in range(first // 128, (last - 1) // 128 + 1):
                low, high = max(first - 128 * j, 0), min(last - 128 * j, 128)
                part = jnp.where((lane >= low) & (lane < high), turned, 0.0)
                tiles[j] = part if tiles[j] is None else tiles[j] + part
    zero = jnp.zeros((piece.shape[0], 128), jnp.float32)
    return [zero if tile is None else tile for tile in tiles]


def one_hot(wanted, source):
    return jnp.where(wanted == source, 1.0, 0.0).astype(jnp.bfloat16)


def pack(block, slots, unknowns):
    span, used = block.shape[0], slots * unknowns
    lane = lax.broadcasted_iota(jnp.int32, (span, 128), 1)
    rest = block[:, 128:].astype(jnp.float32)
    turned = pltpu.roll(rest, 64, 1)
    zero = jnp.zeros_like(rest)
    parts = [jnp.where(lane < 64, rest, zero), jnp.where(lane < 64, zero, turned), jnp.where(lane < 64, turned, rest)]
    stacked = jnp.concatenate([block[:, :128]] + [part.astype(jnp.bfloat16) for part in parts], axis=0)
    row = lax.broadcasted_iota(jnp.int32, (PACK, 4 * span), 0)
    source = lax.broadcasted_iota(jnp.int32, (PACK, 4 * span), 1)
    part, at = source // span, source % span
    dense = at // SLOT * unknowns + at % SLOT
    dense = jnp.where(at % SLOT < unknowns, dense, -1)
    half = used // 2
    low = jnp.where((dense >= 0) & (dense < half), used + dense, -1)
    high = jnp.where(dense >= half, used + dense - half, -1)
    mark = jnp.where(at % SLOT == 0, used + half + at // SLOT, -1)
    goes = jnp.where(part == 0, dense, jnp.where(part == 1, low, jnp.where(part == 2, high, mark)))
    return jnp.dot(one_hot(goes, row), stacked, preferred_element_type=jnp.float32).astype(jnp.bfloat16)


def unpack(packed, slots, unknowns):
    span, used = slots * SLOT, slots * unknowns
    row = lax.broadcasted_iota(jnp.int32, (3 * span, PACK), 0)
    source = lax.broadcasted_iota(jnp.int32, (3 * span, PACK), 1)
    part, at = row // span, row % span
    dense = at // SLOT * unknowns + at % SLOT
    half = used // 2
    folded = used + jnp.where(dense < half, dense, dense - half)
    comes = jnp.where(part == 0, dense, jnp.where(part == 1, folded, used + half + at // SLOT))
    comes = jnp.where((at % SLOT < unknowns) | (part == 2), comes, -1)
    laid = jnp.dot(one_hot(comes, source), packed, preferred_element_type=jnp.float32)
    lane = lax.broadcasted_iota(jnp.int32, (span, 128), 1)
    at = lax.broadcasted_iota(jnp.int32, (span, 128), 0)
    rest = laid[span : 2 * span]
    rest = jnp.where(at // SLOT * unknowns + at % SLOT < half, rest, pltpu.roll(rest, 64, 1))
    rest = jnp.where(lane < 64, rest, laid[2 * span :] + (at % SLOT).astype(jnp.float32))
    return laid[:span].astype(jnp.bfloat16), rest.astype(jnp.bfloat16)


def kernel(
    a_ref, a_codes, p_ref, p_codes, out_ref,
    a_buf, p_buf, mid, inner_side, outer_side, packed, got, rows_w, own, send_y, got_y, send_x, got_x,
    a_sem, p_sem, side_out, side_in, mid_out, mid_in, y_out, y_in, x_out, x_in, ready,
):
    tile_x, tile_y, slots_a, edges, _ = a_ref.shape
    slots_p, unknowns = p_ref.shape[1], p_ref.shape[2]
    span = slots_p * SLOT
    at_x, at_y = lax.axis_index("gx"), lax.axis_index("gy")
    count_x, count_y = lax.axis_size("gx"), lax.axis_size("gy")
    outer = at_y % 2
    inner = 1 - outer
    rows = (inner, outer)
    sides = (inner_side, outer_side)

    def inside(step_x, step_y):
        there_x, there_y = at_x + step_x, at_y + step_y
        return (there_x >= 0) & (there_x < count_x) & (there_y >= 0) & (there_y < count_y)

    p_copy = pltpu.make_async_copy(p_ref, p_buf, p_sem)
    p_copy.start()
    def start_order(x, y):
        z = y // 2 % 4 * 4 + x // 4
        return (jnp.where(z < 8, 2 * z, jnp.where(z < 12, 16, 15)) + x % 4 + y // 8) * 1024 + x * 32 + y

    def later(step_x, step_y):
        return start_order(at_x + step_x, at_y + step_y) > start_order(at_x, at_y)

    barrier = pltpu.get_barrier_semaphore()
    earlier_ones = jnp.int32(0)
    for step_x, step_y in WAYS:
        there = inside(step_x, step_y)
        comes_later = later(step_x, step_y)
        earlier_ones += (there & jnp.logical_not(comes_later)).astype(jnp.int32)

        @pl.when(there & comes_later)
        def _():
            pl.semaphore_signal(
                barrier, inc=1, device_id=(at_x + step_x, at_y + step_y), device_id_type=pl.DeviceIdType.MESH
            )

    def a_copy(x, y):
        return pltpu.make_async_copy(a_ref.at[x, y], a_buf.at[x, y], a_sem.at[x, y])

    for y in (inner, outer):
        for x in range(tile_x):
            a_copy(x, y).start()

    for way in range(2):
        @pl.when(jnp.logical_not(inside(1 - 2 * way, 0)))
        def _():
            column = (tile_x + 1) * (1 - way)
            mid[:, column] = jnp.zeros((tile_y, span, WIDE), jnp.bfloat16)
            got_x[way] = jnp.zeros(got_x.shape[1:], got_x.dtype)

    for side in range(2):
        step_y = 2 * rows[side] - 1
        for step_x in (-1, 0, 1):
            @pl.when(jnp.logical_not(inside(step_x, step_y)))
            def _():
                columns = {0: slice(1, tile_x + 1), -1: slice(0, 1), 1: slice(tile_x + 1, tile_x + 2)}[step_x]
                holds = got if side else inner_side
                holds[columns] = jnp.zeros_like(holds[columns])
                if step_x == 0:
                    got_y[side] = jnp.zeros(got_y.shape[1:], got_y.dtype)

    rows_w[:, :, :, :, edges:] = jnp.zeros((tile_x, tile_y, slots_a, 2 * span, WIDE - edges), jnp.bfloat16)

    pl.when(earlier_ones > 0)(lambda: pl.semaphore_wait(barrier, earlier_ones))
    for step_x, step_y in WAYS:
        @pl.when(inside(step_x, step_y) & jnp.logical_not(later(step_x, step_y)))
        def _():
            pl.semaphore_signal(
                ready.at[(1 - step_x) * 3 + 1 - step_y],
                inc=1,
                device_id=(at_x + step_x, at_y + step_y),
                device_id_type=pl.DeviceIdType.MESH,
            )

    p_copy.wait()
    taken = slots_p * unknowns * tile_y
    target_row = lax.broadcasted_iota(jnp.int32, (tile_y * span, taken), 0)
    source_row = lax.broadcasted_iota(jnp.int32, (tile_y * span, taken), 1)
    row = lax.broadcasted_iota(jnp.int32, (span, WIDE - edges), 0)
    for x in range(tile_x):
        wanted = jnp.full_like(target_row, -1)
        for y in range(tile_y):
            place = row % SLOT
            for m in range(slots_p):
                code = p_codes[m, y, x]
                first_row = y * span + m * SLOT
                fits = (target_row >= first_row) & (target_row < first_row + unknowns) & (code < 5)
                wanted = jnp.where(fits, (target_row - first_row + m * unknowns) * tile_y + y, wanted)
                shift = jnp.where(code == 1, -5, jnp.where(code == 2, 5, jnp.where(code == 3, -1, jnp.where(code == 4, 1, 0))))
                place = place + jnp.where(row // SLOT == m, shift * unknowns, 0)
            mid[y, x + 1, :, edges:] = place.astype(jnp.float32).astype(jnp.bfloat16)
        order = jnp.where(wanted == source_row, 1.0, 0.0).astype(jnp.bfloat16)
        laid = jnp.dot(order, p_buf[x].reshape(taken, edges), preferred_element_type=jnp.float32).astype(jnp.bfloat16)
        for y in range(tile_y):
            mid[y, x + 1, :, :edges] = laid[y * span : (y + 1) * span]

    def side_copy(step_x, side):
        source = {0: pl.ds(1, tile_x), -1: pl.ds(1, 1), 1: pl.ds(tile_x, 1)}[step_x]
        target = {0: pl.ds(1, tile_x), -1: pl.ds(tile_x + 1, 1), 1: pl.ds(0, 1)}[step_x]
        return pltpu.make_async_remote_copy(
            src_ref=packed.at[pl.ds(source.start - 1, source.size)] if side else mid.at[inner, source],
            dst_ref=(got if side else inner_side).at[target],
            send_sem=side_out.at[side, step_x + 1],
            recv_sem=side_in.at[side, step_x + 1],
            device_id=(at_x + step_x, at_y + 2 * rows[side] - 1),
            device_id_type=pl.DeviceIdType.MESH,
        )

    def mid_copy(way):
        return pltpu.make_async_remote_copy(
            src_ref=mid.at[:, pl.ds(1 + (tile_x - 1) * way, 1)],
            dst_ref=mid.at[:, pl.ds((tile_x + 1) * (1 - way), 1)],
            send_sem=mid_out.at[way],
            recv_sem=mid_in.at[way],
            device_id=(at_x + 2 * way - 1, at_y),
            device_id_type=pl.DeviceIdType.MESH,
        )

    def y_copy(side):
        return pltpu.make_async_remote_copy(
            src_ref=send_y.at[side],
            dst_ref=got_y.at[side],
            send_sem=y_out.at[side],
            recv_sem=y_in.at[side],
            device_id=(at_x, at_y + 2 * rows[side] - 1),
            device_id_type=pl.DeviceIdType.MESH,
        )

    def x_copy(way, side):
        return pltpu.make_async_remote_copy(
            src_ref=send_x.at[way, side],
            dst_ref=got_x.at[way, side],
            send_sem=x_out.at[way, side],
            recv_sem=x_in.at[way, side],
            device_id=(at_x + 2 * way - 1, at_y),
            device_id_type=pl.DeviceIdType.MESH,
        )

    def when_inside(step_x, step_y, does):
        pl.when(inside(step_x, step_y))(does)

    def first(y):
        for x in range(tile_x):
            a_copy(x, y).wait()
            here = mid[y, x + 1, :, :edges]
            for k in range(slots_a):
                product = jnp.dot(here, a_buf[x, y, k], preferred_element_type=jnp.float32)
                high = product.astype(jnp.bfloat16)
                rows_w[x, y, k, :span, :edges] = high
                rows_w[x, y, k, span:, :edges] = (product - high.astype(jnp.float32)).astype(jnp.bfloat16)

    lane = lax.broadcasted_iota(jnp.int32, (span, COLS), 1).astype(jnp.float32)

    def second(side):
        y = rows[side]
        for x in range(tile_x):
            summed = jnp.zeros((span, COLS), jnp.float32)
            for k in range(slots_a):
                code = a_codes[x, y, k]
                live = code < 9
                code = jnp.where(live, code, 4)
                step_x, step_y = code // 3 - 1, code % 3 - 1
                there = jnp.where(
                    step_y == 2 * y - 1,
                    sides[side][x + 1 + step_x],
                    mid[jnp.clip(y + step_y, 0, tile_y - 1), x + 1 + step_x],
                )
                base = jnp.where(live, unknowns * (5 * (step_x + 2) + step_y + 2), -4096).astype(jnp.float32)
                both = lax.dot_general(
                    rows_w[x, y, k], there, (((1,), (1,)), ((), ())), preferred_element_type=jnp.float32
                )
                block = (both[:span] + both[span:]).astype(jnp.bfloat16)
                target = there[:, edges : edges + 1].astype(jnp.float32) + base
                chosen = jnp.where(lane == target, 1.0, 0.0).astype(jnp.bfloat16)
                summed += jnp.dot(block, chosen, preferred_element_type=jnp.float32)
            own[0, x, y] = summed[:SLOT]
            for q in range(1, 5):
                value = jnp.zeros((SLOT, COLS), jnp.float32)
                for m in range(1, slots_p):
                    value += jnp.where(p_codes[m, y, x] == q, summed[SLOT * m : SLOT * (m + 1)], 0.0)
                own[q, x, y] = value

    def send_contributions(side):
        y = rows[side]
        for x in range(tile_x):
            send_y[side, x] = own[y + 3, x, y].astype(jnp.bfloat16)
        when_inside(0, 2 * y - 1, lambda: y_copy(side).start())
        for way in range(2):
            send_x[way, side] = own[way + 1, (tile_x - 1) * way, y].astype(jnp.bfloat16)
            when_inside(2 * way - 1, 0, lambda: x_copy(way, side).start())

    for x in range(tile_x):
        packed[x] = pack(mid[outer, x + 1], slots_p, unknowns)

    outer_copies = [(step_x, 2 * outer - 1, functools.partial(side_copy, step_x, 1)) for step_x in (0, -1, 1)]
    inner_copies = [(step_x, 2 * inner - 1, functools.partial(side_copy, step_x, 0)) for step_x in (0, -1, 1)]
    mid_copies = [(2 * way - 1, 0, functools.partial(mid_copy, way)) for way in range(2)]
    for step_x, step_y, copy in outer_copies + mid_copies + inner_copies:
        pl.when(inside(step_x, step_y) & jnp.logical_not(later(step_x, step_y)))(lambda: copy().start())
    for step_x, step_y, copy in mid_copies + inner_copies + outer_copies:
        @pl.when(inside(step_x, step_y) & later(step_x, step_y))
        def _():
            pl.semaphore_wait(ready.at[(step_x + 1) * 3 + step_y + 1], 1)
            copy().start()

    def both_firsts(i, _):
        first(jnp.where(i == 0, inner, outer))
        return 0

    lax.fori_loop(0, 2, both_firsts, 0)

    for way in range(2):
        when_inside(1 - 2 * way, 0, lambda: mid_copy(way).wait_recv())
    for side in range(2):
        for step_x in (0, -1, 1):
            when_inside(-step_x, 2 * rows[side] - 1, lambda: side_copy(step_x, side).wait_recv())
        if side:
            for x in range(tile_x + 2):
                outer_side[x, :, :128], outer_side[x, :, 128:] = unpack(got[x], slots_p, unknowns)
        second(side)
        send_contributions(side)

    def put(x, y, pieces, add):
        total = None
        for piece, face in pieces:
            tiles = spread_out(piece.astype(jnp.float32), FACES[face], unknowns)
            total = tiles if total is None else [s + t for s, t in zip(total, tiles)]
        for j, tile in enumerate(total):
            high = min(128 * (j + 1), out_ref.shape[3])
            tile = tile[:unknowns, : high - 128 * j]
            if add:
                tile = tile + out_ref[x, y, :, 128 * j : high]
            out_ref[x, y, :, 128 * j : high] = tile

    for x in range(tile_x):
        for y in range(tile_y):
            pieces = []
            for face, (face_x, face_y) in enumerate(FACES):
                from_x, from_y = x - face_x, y - face_y
                if 0 <= from_x < tile_x and 0 <= from_y < tile_y:
                    pieces.append((own[face, from_x, from_y], face))
            put(x, y, pieces, False)

    for way in range(2):
        for side in range(2):
            when_inside(1 - 2 * way, 0, lambda: x_copy(way, side).wait_recv())
    for side in range(2):
        when_inside(0, 2 * rows[side] - 1, lambda: y_copy(side).wait_recv())

    for x in range(tile_x):
        for y in range(tile_y):
            side = outer if y else inner
            pieces = [(got_y[side, x], 4 - y)]
            if x == 0:
                pieces.append((got_x[1, side], 2))
            if x == tile_x - 1:
                pieces.append((got_x[0, side], 1))
            put(x, y, pieces, True)

    for side in range(2):
        for step_x in (-1, 0, 1):
            when_inside(step_x, 2 * rows[side] - 1, lambda: side_copy(step_x, side).wait_send())
        when_inside(0, 2 * rows[side] - 1, lambda: y_copy(side).wait_send())
        for way in range(2):
            when_inside(2 * way - 1, 0, lambda: x_copy(way, side).wait_send())
    for way in range(2):
        when_inside(2 * way - 1, 0, lambda: mid_copy(way).wait_send())


def shards(a_blocks, a_codes, p_blocks, p_codes):
    tile_x, tile_y, slots_a = a_codes.shape
    slots_p, unknowns, edges = p_blocks.shape[2:]
    span = slots_p * SLOT
    dma = pltpu.SemaphoreType.DMA
    return pl.pallas_call(
        kernel,
        out_shape=jax.ShapeDtypeStruct((tile_x, tile_y, unknowns, 49 * unknowns), jnp.float32),
        in_specs=[
            pl.BlockSpec(memory_space=pltpu.HBM),
            pl.BlockSpec(memory_space=pltpu.SMEM),
            pl.BlockSpec(memory_space=pltpu.HBM),
            pl.BlockSpec(memory_space=pltpu.SMEM),
        ],
        out_specs=pl.BlockSpec(memory_space=pltpu.VMEM),
        scratch_shapes=[
            pltpu.VMEM((tile_x, tile_y, slots_a, edges, edges), jnp.bfloat16),
            pltpu.VMEM((tile_x, slots_p, unknowns, tile_y, edges), jnp.bfloat16),
            pltpu.VMEM((tile_y, tile_x + 2, span, WIDE), jnp.bfloat16),
            pltpu.VMEM((tile_x + 2, span, WIDE), jnp.bfloat16),
            pltpu.VMEM((tile_x + 2, span, WIDE), jnp.bfloat16),
            pltpu.VMEM((tile_x, PACK, 128), jnp.bfloat16),
            pltpu.VMEM((tile_x + 2, PACK, 128), jnp.bfloat16),
            pltpu.VMEM((tile_x, tile_y, slots_a, 2 * span, WIDE), jnp.bfloat16),
            pltpu.VMEM((5, tile_x, tile_y, SLOT, COLS), jnp.float32),
            pltpu.VMEM((tile_y, tile_x, SLOT, COLS), jnp.bfloat16),
            pltpu.VMEM((tile_y, tile_x, SLOT, COLS), jnp.bfloat16),
            pltpu.VMEM((2, tile_y, SLOT, COLS), jnp.bfloat16),
            pltpu.VMEM((2, tile_y, SLOT, COLS), jnp.bfloat16),
            dma((tile_x, tile_y)),
            dma,
            dma((2, 3)),
            dma((2, 3)),
            dma((2,)),
            dma((2,)),
            dma((2,)),
            dma((2,)),
            dma((2, 2)),
            dma((2, 2)),
            pltpu.SemaphoreType.REGULAR((9,)),
        ],
        compiler_params=pltpu.CompilerParams(
            collective_id=0, has_side_effects=True, vmem_limit_bytes=40 * 2**20
        ),
    )(pltpu.with_memory_space_constraint(a_blocks, pltpu.HBM), pltpu.with_memory_space_constraint(a_codes, pltpu.HBM), pltpu.with_memory_space_constraint(jnp.transpose(p_blocks, (0, 2, 3, 1, 4)), pltpu.HBM), pltpu.with_memory_space_constraint(jnp.transpose(p_codes, (2, 1, 0)), pltpu.HBM))


def solution(mesh):
    in_specs = (
        P("gx", "gy", None, None, None),
        P("gx", "gy", None),
        P("gx", "gy", None, None, None),
        P("gx", "gy", None),
    )
    out_specs = P("gx", "gy", None, None)
    return jax.shard_map(shards, mesh=mesh, in_specs=in_specs, out_specs=out_specs, check_vma=False)
```

```python
import functools

import jax
import jax.numpy as jnp
from jax import lax
from jax.experimental import pallas as pl
from jax.experimental.pallas import tpu as pltpu
from jax.sharding import PartitionSpec as P

WAYS = ((-1, 0), (1, 0), (0, -1), (0, 1), (-1, -1), (-1, 1), (1, -1), (1, 1))
FACES = ((0, 0), (-1, 0), (1, 0), (0, -1), (0, 1))
SLOT = 16
WIDE = 256
PACK = 64
COLS = 384


def spread_out(piece, face, unknowns):
    face_x, face_y = face
    lane = lax.broadcasted_iota(jnp.int32, (piece.shape[0], 128), 1)
    tiles = [None] * 5
    for step in range(5):
        source = 5 * unknowns * step
        target = 7 * unknowns * (step + 1 - face_x) + unknowns * (1 - face_y)
        width = 5 * unknowns
        for i in range(source // 128, (source + width - 1) // 128 + 1):
            turned = piece[:, 128 * i : 128 * (i + 1)]
            turn = (target - source) % 128
            if turn:
                turned = pltpu.roll(turned, turn, 1)
            first = max(source, 128 * i) - source + target
            last = min(source + width, 128 * (i + 1)) - source + target
            for j in range(first // 128, (last - 1) // 128 + 1):
                low, high = max(first - 128 * j, 0), min(last - 128 * j, 128)
                part = jnp.where((lane >= low) & (lane < high), turned, 0.0)
                tiles[j] = part if tiles[j] is None else tiles[j] + part
    zero = jnp.zeros((piece.shape[0], 128), jnp.float32)
    return [zero if tile is None else tile for tile in tiles]


def one_hot(wanted, source):
    return jnp.where(wanted == source, 1.0, 0.0).astype(jnp.bfloat16)


def pack(block, slots, unknowns):
    span, used = block.shape[0], slots * unknowns
    lane = lax.broadcasted_iota(jnp.int32, (span, 128), 1)
    rest = block[:, 128:].astype(jnp.float32)
    turned = pltpu.roll(rest, 64, 1)
    zero = jnp.zeros_like(rest)
    parts = [jnp.where(lane < 64, rest, zero), jnp.where(lane < 64, zero, turned), jnp.where(lane < 64, turned, rest)]
    stacked = jnp.concatenate([block[:, :128]] + [part.astype(jnp.bfloat16) for part in parts], axis=0)
    row = lax.broadcasted_iota(jnp.int32, (PACK, 4 * span), 0)
    source = lax.broadcasted_iota(jnp.int32, (PACK, 4 * span), 1)
    part, at = source // span, source % span
    dense = at // SLOT * unknowns + at % SLOT
    dense = jnp.where(at % SLOT < unknowns, dense, -1)
    half = used // 2
    low = jnp.where((dense >= 0) & (dense < half), used + dense, -1)
    high = jnp.where(dense >= half, used + dense - half, -1)
    mark = jnp.where(at % SLOT == 0, used + half + at // SLOT, -1)
    goes = jnp.where(part == 0, dense, jnp.where(part == 1, low, jnp.where(part == 2, high, mark)))
    return jnp.dot(one_hot(goes, row), stacked, preferred_element_type=jnp.float32).astype(jnp.bfloat16)


def unpack(packed, slots, unknowns):
    span, used = slots * SLOT, slots * unknowns
    row = lax.broadcasted_iota(jnp.int32, (3 * span, PACK), 0)
    source = lax.broadcasted_iota(jnp.int32, (3 * span, PACK), 1)
    part, at = row // span, row % span
    dense = at // SLOT * unknowns + at % SLOT
    half = used // 2
    folded = used + jnp.where(dense < half, dense, dense - half)
    comes = jnp.where(part == 0, dense, jnp.where(part == 1, folded, used + half + at // SLOT))
    comes = jnp.where((at % SLOT < unknowns) | (part == 2), comes, -1)
    laid = jnp.dot(one_hot(comes, source), packed, preferred_element_type=jnp.float32)
    lane = lax.broadcasted_iota(jnp.int32, (span, 128), 1)
    at = lax.broadcasted_iota(jnp.int32, (span, 128), 0)
    rest = laid[span : 2 * span]
    rest = jnp.where(at // SLOT * unknowns + at % SLOT < half, rest, pltpu.roll(rest, 64, 1))
    rest = jnp.where(lane < 64, rest, laid[2 * span :] + (at % SLOT).astype(jnp.float32))
    return laid[:span].astype(jnp.bfloat16), rest.astype(jnp.bfloat16)


def kernel(
    a_ref, a_codes, p_ref, p_codes, out_ref,
    a_buf, p_buf, mid, inner_side, outer_side, packed, got, half, half_sent, half_got, rows_w, turned_w, own, send_y, got_y, send_x, got_x,
    a_sem, p_sem, side_out, side_in, mid_out, mid_in, y_out, y_in, x_out, x_in, half_out, half_in, ready,
):
    tile_x, tile_y, slots_a, edges, _ = a_ref.shape
    slots_p, unknowns = p_ref.shape[1], p_ref.shape[2]
    span = slots_p * SLOT
    at_x, at_y = lax.axis_index("gx"), lax.axis_index("gy")
    count_x, count_y = lax.axis_size("gx"), lax.axis_size("gy")
    outer = at_y % 2
    inner = 1 - outer
    rows = (inner, outer)
    sides = (inner_side, outer_side)

    def inside(step_x, step_y):
        there_x, there_y = at_x + step_x, at_y + step_y
        return (there_x >= 0) & (there_x < count_x) & (there_y >= 0) & (there_y < count_y)

    p_copy = pltpu.make_async_copy(p_ref, p_buf, p_sem)
    p_copy.start()
    def start_order(x, y):
        z = y // 2 % 4 * 4 + x // 4
        return (jnp.where(z < 8, 2 * z, jnp.where(z < 12, 16, 15)) + x % 4 + y // 8) * 1024 + x * 32 + y

    def later(step_x, step_y):
        return start_order(at_x + step_x, at_y + step_y) > start_order(at_x, at_y)

    barrier = pltpu.get_barrier_semaphore()
    earlier_ones = jnp.int32(0)
    for step_x, step_y in WAYS:
        there = inside(step_x, step_y)
        comes_later = later(step_x, step_y)
        earlier_ones += (there & jnp.logical_not(comes_later)).astype(jnp.int32)

        @pl.when(there & comes_later)
        def _():
            pl.semaphore_signal(
                barrier, inc=1, device_id=(at_x + step_x, at_y + step_y), device_id_type=pl.DeviceIdType.MESH
            )

    def a_copy(x, y):
        return pltpu.make_async_copy(a_ref.at[x, y], a_buf.at[x, y], a_sem.at[x, y])

    for y in (outer, inner):
        for x in range(tile_x):
            a_copy(x, y).start()

    for way in range(2):
        @pl.when(jnp.logical_not(inside(1 - 2 * way, 0)))
        def _():
            column = (tile_x + 1) * (1 - way)
            mid[:, column] = jnp.zeros((tile_y, span, WIDE), jnp.bfloat16)
            got_x[way] = jnp.zeros(got_x.shape[1:], got_x.dtype)

    for side in range(2):
        step_y = 2 * rows[side] - 1
        for step_x in (-1, 0, 1):
            @pl.when(jnp.logical_not(inside(step_x, step_y)))
            def _():
                columns = {0: slice(1, tile_x + 1), -1: slice(0, 1), 1: slice(tile_x + 1, tile_x + 2)}[step_x]
                holds = got if side else inner_side
                holds[columns] = jnp.zeros_like(holds[columns])
                if step_x == 0:
                    got_y[side] = jnp.zeros(got_y.shape[1:], got_y.dtype)
                    if side:
                        half_got[...] = jnp.zeros_like(half_got)

    rows_w[:, :, :, :, edges:] = jnp.zeros((tile_x, tile_y, slots_a, 2 * span, WIDE - edges), jnp.bfloat16)
    turned_w[:, :, :, edges:] = jnp.zeros((tile_x, 3, 2 * span, WIDE - edges), jnp.bfloat16)
    half[:, :, edges:] = jnp.zeros((tile_x, span, WIDE - edges), jnp.bfloat16)

    pl.when(earlier_ones > 0)(lambda: pl.semaphore_wait(barrier, earlier_ones))
    for step_x, step_y in WAYS:
        @pl.when(inside(step_x, step_y) & jnp.logical_not(later(step_x, step_y)))
        def _():
            pl.semaphore_signal(
                ready.at[(1 - step_x) * 3 + 1 - step_y],
                inc=1,
                device_id=(at_x + step_x, at_y + step_y),
                device_id_type=pl.DeviceIdType.MESH,
            )

    p_copy.wait()
    taken = slots_p * unknowns * tile_y
    target_row = lax.broadcasted_iota(jnp.int32, (tile_y * span, taken), 0)
    source_row = lax.broadcasted_iota(jnp.int32, (tile_y * span, taken), 1)
    row = lax.broadcasted_iota(jnp.int32, (span, WIDE - edges), 0)
    for x in range(tile_x):
        wanted = jnp.full_like(target_row, -1)
        for y in range(tile_y):
            place = row % SLOT
            for m in range(slots_p):
                code = p_codes[m, y, x]
                first_row = y * span + m * SLOT
                fits = (target_row >= first_row) & (target_row < first_row + unknowns) & (code < 5)
                wanted = jnp.where(fits, (target_row - first_row + m * unknowns) * tile_y + y, wanted)
                shift = jnp.where(code == 1, -5, jnp.where(code == 2, 5, jnp.where(code == 3, -1, jnp.where(code == 4, 1, 0))))
                place = place + jnp.where(row // SLOT == m, shift * unknowns, 0)
            mid[y, x + 1, :, edges:] = place.astype(jnp.float32).astype(jnp.bfloat16)
        order = jnp.where(wanted == source_row, 1.0, 0.0).astype(jnp.bfloat16)
        laid = jnp.dot(order, p_buf[x].reshape(taken, edges), preferred_element_type=jnp.float32).astype(jnp.bfloat16)
        for y in range(tile_y):
            mid[y, x + 1, :, :edges] = laid[y * span : (y + 1) * span]

    def side_copy(step_x, side):
        source = {0: pl.ds(1, tile_x), -1: pl.ds(1, 1), 1: pl.ds(tile_x, 1)}[step_x]
        target = {0: pl.ds(1, tile_x), -1: pl.ds(tile_x + 1, 1), 1: pl.ds(0, 1)}[step_x]
        return pltpu.make_async_remote_copy(
            src_ref=packed.at[pl.ds(source.start - 1, source.size)] if side else mid.at[inner, source],
            dst_ref=(got if side else inner_side).at[target],
            send_sem=side_out.at[side, step_x + 1],
            recv_sem=side_in.at[side, step_x + 1],
            device_id=(at_x + step_x, at_y + 2 * rows[side] - 1),
            device_id_type=pl.DeviceIdType.MESH,
        )

    def mid_copy(way):
        return pltpu.make_async_remote_copy(
            src_ref=mid.at[:, pl.ds(1 + (tile_x - 1) * way, 1)],
            dst_ref=mid.at[:, pl.ds((tile_x + 1) * (1 - way), 1)],
            send_sem=mid_out.at[way],
            recv_sem=mid_in.at[way],
            device_id=(at_x + 2 * way - 1, at_y),
            device_id_type=pl.DeviceIdType.MESH,
        )

    def y_copy(side):
        return pltpu.make_async_remote_copy(
            src_ref=send_y.at[side],
            dst_ref=got_y.at[side],
            send_sem=y_out.at[side],
            recv_sem=y_in.at[side],
            device_id=(at_x, at_y + 2 * rows[side] - 1),
            device_id_type=pl.DeviceIdType.MESH,
        )

    def x_copy(way, side):
        return pltpu.make_async_remote_copy(
            src_ref=send_x.at[way, side],
            dst_ref=got_x.at[way, side],
            send_sem=x_out.at[way, side],
            recv_sem=x_in.at[way, side],
            device_id=(at_x + 2 * way - 1, at_y),
            device_id_type=pl.DeviceIdType.MESH,
        )

    def half_copy():
        return pltpu.make_async_remote_copy(
            src_ref=half_sent,
            dst_ref=half_got,
            send_sem=half_out,
            recv_sem=half_in,
            device_id=(at_x, at_y + 2 * outer - 1),
            device_id_type=pl.DeviceIdType.MESH,
        )

    def when_inside(step_x, step_y, does):
        pl.when(inside(step_x, step_y))(does)

    def first(side):
        y = rows[side]
        for x in range(tile_x):
            a_copy(x, y).wait()
            here = mid[y, x + 1, :, :edges]
            outward = [jnp.zeros((2 * span, edges), jnp.bfloat16)] * 3
            for k in range(slots_a):
                product = jnp.dot(here, a_buf[x, y, k], preferred_element_type=jnp.float32)
                high = product.astype(jnp.bfloat16)
                low = (product - high.astype(jnp.float32)).astype(jnp.bfloat16)
                both = jnp.concatenate([high, low], axis=0)
                rows_w[x, y, k, :, :edges] = both
                if side:
                    code = a_codes[x, y, k]
                    outward = [jnp.where(code == 3 * i + 2 * y, both, value) for i, value in enumerate(outward)]
            if side:
                for i, value in enumerate(outward):
                    turned_w[x, i, :, :edges] = value
                    leaves = jnp.zeros((SLOT, edges), jnp.bfloat16)
                    for m in range(1, slots_p):
                        leaves = jnp.where(p_codes[m, y, x] == y + 3, value[SLOT * m : SLOT * (m + 1)], leaves)
                    half[x, SLOT * i : SLOT * (i + 1), :edges] = leaves
                half_sent[x] = pack(half[x], slots_p, unknowns)

    lane = lax.broadcasted_iota(jnp.int32, (span, COLS), 1).astype(jnp.float32)

    def placed(block, there, base):
        target = there[:, edges : edges + 1].astype(jnp.float32) + base
        chosen = jnp.where(lane == target, 1.0, 0.0).astype(jnp.bfloat16)
        return jnp.dot(block.astype(jnp.bfloat16), chosen, preferred_element_type=jnp.float32)

    def across(left, there):
        return lax.dot_general(left, there, (((1,), (1,)), ((), ())), preferred_element_type=jnp.float32)

    def store(x, y, summed, add):
        def put_own(q, value):
            own[q, x, y] = own[q, x, y] + value if add else value

        put_own(0, summed[:SLOT])
        for q in range(1, 5):
            value = jnp.zeros((SLOT, COLS), jnp.float32)
            for m in range(1, slots_p):
                value += jnp.where(p_codes[m, y, x] == q, summed[SLOT * m : SLOT * (m + 1)], 0.0)
            put_own(q, value)

    def second(side):
        y = rows[side]
        for x in range(tile_x):
            summed = jnp.zeros((span, COLS), jnp.float32)
            for k in range(slots_a):
                code = a_codes[x, y, k]
                live = code < 9
                code = jnp.where(live, code, 4)
                step_x, step_y = code // 3 - 1, code % 3 - 1
                away = step_y == 2 * y - 1
                there = mid[jnp.clip(y + step_y, 0, tile_y - 1), x + 1 + step_x]
                if side:
                    live = live & jnp.logical_not(away)
                else:
                    there = jnp.where(away, inner_side[x + 1 + step_x], there)
                base = jnp.where(live, unknowns * (5 * (step_x + 2) + step_y + 2), -4096).astype(jnp.float32)
                both = across(rows_w[x, y, k], there)
                summed += placed(both[:span] + both[span:], there, base)
            store(x, y, summed, False)

    def second_outward():
        for x in range(tile_x):
            summed = jnp.zeros((span, COLS), jnp.float32)
            for i in range(3):
                there = outer_side[x + i]
                base = (unknowns * (5 * (i + 1) + 2 * outer + 1)).astype(jnp.float32)
                both = across(turned_w[x, i], there)
                summed += placed(both[:span] + both[span:], there, base)
            store(x, outer, summed, True)

    def second_inward(x):
        high, rest = unpack(half_got[x], slots_p, unknowns)
        rest = jnp.where(lax.broadcasted_iota(jnp.int32, rest.shape, 1) < edges - 128, rest, jnp.zeros_like(rest))
        left = jnp.concatenate([high, rest], axis=1)
        summed = jnp.zeros((SLOT, COLS), jnp.float32)
        for i in range(3):
            there = mid[outer, x + i]
            product = across(left[SLOT * i : SLOT * (i + 1)], there)
            summed += placed(product, there, float(unknowns * (5 * (i + 1) + 2)))
        return summed

    def send_y_contributions(side):
        y = rows[side]
        for x in range(tile_x):
            send_y[side, x] = own[y + 3, x, y].astype(jnp.bfloat16)
        when_inside(0, 2 * y - 1, lambda: y_copy(side).start())

    def send_x_contributions(side):
        y = rows[side]
        for way in range(2):
            send_x[way, side] = own[way + 1, (tile_x - 1) * way, y].astype(jnp.bfloat16)
            when_inside(2 * way - 1, 0, lambda: x_copy(way, side).start())

    for x in range(tile_x):
        packed[x] = pack(mid[outer, x + 1], slots_p, unknowns)

    outer_copies = [(step_x, 2 * outer - 1, functools.partial(side_copy, step_x, 1)) for step_x in (0, -1, 1)]
    inner_copies = [(step_x, 2 * inner - 1, functools.partial(side_copy, step_x, 0)) for step_x in (0, -1, 1)]
    mid_copies = [(2 * way - 1, 0, functools.partial(mid_copy, way)) for way in range(2)]
    for step_x, step_y, copy in outer_copies + mid_copies + inner_copies:
        pl.when(inside(step_x, step_y) & jnp.logical_not(later(step_x, step_y)))(lambda: copy().start())
    for step_x, step_y, copy in mid_copies + inner_copies + outer_copies:
        @pl.when(inside(step_x, step_y) & later(step_x, step_y))
        def _():
            pl.semaphore_wait(ready.at[(step_x + 1) * 3 + step_y + 1], 1)
            copy().start()

    first(1)
    when_inside(0, 2 * outer - 1, lambda: half_copy().start())
    for way in range(2):
        when_inside(1 - 2 * way, 0, lambda: mid_copy(way).wait_recv())
    second(1)
    send_y_contributions(1)

    first(0)
    for step_x in (0, -1, 1):
        when_inside(-step_x, 2 * inner - 1, lambda: side_copy(step_x, 0).wait_recv())
    second(0)
    send_y_contributions(0)
    send_x_contributions(0)

    def put(x, y, pieces, add):
        total = None
        for piece, face in pieces:
            tiles = spread_out(piece.astype(jnp.float32), FACES[face], unknowns)
            total = tiles if total is None else [s + t for s, t in zip(total, tiles)]
        for j, tile in enumerate(total):
            high = min(128 * (j + 1), out_ref.shape[3])
            tile = tile[:unknowns, : high - 128 * j]
            if add:
                tile = tile + out_ref[x, y, :, 128 * j : high]
            out_ref[x, y, :, 128 * j : high] = tile

    for step_x in (0, -1, 1):
        when_inside(-step_x, 2 * outer - 1, lambda: side_copy(step_x, 1).wait_recv())
    for x in range(tile_x + 2):
        outer_side[x, :, :128], outer_side[x, :, 128:] = unpack(got[x], slots_p, unknowns)
    second_outward()
    send_x_contributions(1)

    for x in range(tile_x):
        for y in range(tile_y):
            pieces = []
            for face, (face_x, face_y) in enumerate(FACES):
                from_x, from_y = x - face_x, y - face_y
                if 0 <= from_x < tile_x and 0 <= from_y < tile_y:
                    pieces.append((own[face, from_x, from_y], face))
            put(x, y, pieces, False)

    when_inside(0, 2 * outer - 1, lambda: half_copy().wait_recv())
    for x in range(tile_x):
        put(x, outer, [(second_inward(x), 0)], True)

    for way in range(2):
        for side in range(2):
            when_inside(1 - 2 * way, 0, lambda: x_copy(way, side).wait_recv())
    for side in range(2):
        when_inside(0, 2 * rows[side] - 1, lambda: y_copy(side).wait_recv())

    for x in range(tile_x):
        for y in range(tile_y):
            side = outer if y else inner
            pieces = [(got_y[side, x], 4 - y)]
            if x == 0:
                pieces.append((got_x[1, side], 2))
            if x == tile_x - 1:
                pieces.append((got_x[0, side], 1))
            put(x, y, pieces, True)

    for side in range(2):
        for step_x in (-1, 0, 1):
            when_inside(step_x, 2 * rows[side] - 1, lambda: side_copy(step_x, side).wait_send())
        when_inside(0, 2 * rows[side] - 1, lambda: y_copy(side).wait_send())
        for way in range(2):
            when_inside(2 * way - 1, 0, lambda: x_copy(way, side).wait_send())
    for way in range(2):
        when_inside(2 * way - 1, 0, lambda: mid_copy(way).wait_send())
    when_inside(0, 2 * outer - 1, lambda: half_copy().wait_send())


def shards(a_blocks, a_codes, p_blocks, p_codes):
    tile_x, tile_y, slots_a = a_codes.shape
    slots_p, unknowns, edges = p_blocks.shape[2:]
    span = slots_p * SLOT
    dma = pltpu.SemaphoreType.DMA
    return pl.pallas_call(
        kernel,
        out_shape=jax.ShapeDtypeStruct((tile_x, tile_y, unknowns, 49 * unknowns), jnp.float32),
        in_specs=[
            pl.BlockSpec(memory_space=pltpu.HBM),
            pl.BlockSpec(memory_space=pltpu.SMEM),
            pl.BlockSpec(memory_space=pltpu.HBM),
            pl.BlockSpec(memory_space=pltpu.SMEM),
        ],
        out_specs=pl.BlockSpec(memory_space=pltpu.VMEM),
        scratch_shapes=[
            pltpu.VMEM((tile_x, tile_y, slots_a, edges, edges), jnp.bfloat16),
            pltpu.VMEM((tile_x, slots_p, unknowns, tile_y, edges), jnp.bfloat16),
            pltpu.VMEM((tile_y, tile_x + 2, span, WIDE), jnp.bfloat16),
            pltpu.VMEM((tile_x + 2, span, WIDE), jnp.bfloat16),
            pltpu.VMEM((tile_x + 2, span, WIDE), jnp.bfloat16),
            pltpu.VMEM((tile_x, PACK, 128), jnp.bfloat16),
            pltpu.VMEM((tile_x + 2, PACK, 128), jnp.bfloat16),
            pltpu.VMEM((tile_x, span, WIDE), jnp.bfloat16),
            pltpu.VMEM((tile_x, PACK, 128), jnp.bfloat16),
            pltpu.VMEM((tile_x, PACK, 128), jnp.bfloat16),
            pltpu.VMEM((tile_x, tile_y, slots_a, 2 * span, WIDE), jnp.bfloat16),
            pltpu.VMEM((tile_x, 3, 2 * span, WIDE), jnp.bfloat16),
            pltpu.VMEM((5, tile_x, tile_y, SLOT, COLS), jnp.float32),
            pltpu.VMEM((tile_y, tile_x, SLOT, COLS), jnp.bfloat16),
            pltpu.VMEM((tile_y, tile_x, SLOT, COLS), jnp.bfloat16),
            pltpu.VMEM((2, tile_y, SLOT, COLS), jnp.bfloat16),
            pltpu.VMEM((2, tile_y, SLOT, COLS), jnp.bfloat16),
            dma((tile_x, tile_y)),
            dma,
            dma((2, 3)),
            dma((2, 3)),
            dma((2,)),
            dma((2,)),
            dma((2,)),
            dma((2,)),
            dma((2, 2)),
            dma((2, 2)),
            dma,
            dma,
            pltpu.SemaphoreType.REGULAR((9,)),
        ],
        compiler_params=pltpu.CompilerParams(
            collective_id=0, has_side_effects=True, vmem_limit_bytes=40 * 2**20
        ),
    )(pltpu.with_memory_space_constraint(a_blocks, pltpu.HBM), pltpu.with_memory_space_constraint(a_codes, pltpu.HBM), pltpu.with_memory_space_constraint(jnp.transpose(p_blocks, (0, 2, 3, 1, 4)), pltpu.HBM), pltpu.with_memory_space_constraint(jnp.transpose(p_codes, (2, 1, 0)), pltpu.HBM))


def solution(mesh):
    in_specs = (
        P("gx", "gy", None, None, None),
        P("gx", "gy", None),
        P("gx", "gy", None, None, None),
        P("gx", "gy", None),
    )
    out_specs = P("gx", "gy", None, None)
    return jax.shard_map(shards, mesh=mesh, in_specs=in_specs, out_specs=out_specs, check_vma=False)
```

```python
import functools

import jax
import jax.numpy as jnp
from jax import lax
from jax.experimental import pallas as pl
from jax.experimental.pallas import tpu as pltpu
from jax.sharding import PartitionSpec as P

WAYS = ((-1, 0), (1, 0), (0, -1), (0, 1), (-1, -1), (-1, 1), (1, -1), (1, 1))
FACES = ((0, 0), (-1, 0), (1, 0), (0, -1), (0, 1))
SLOT = 16
WIDE = 256
PACK = 64
COLS = 384


def spread_out(piece, face, unknowns):
    face_x, face_y = face
    lane = lax.broadcasted_iota(jnp.int32, (piece.shape[0], 128), 1)
    tiles = [None] * 5
    for step in range(5):
        source = 5 * unknowns * step
        target = 7 * unknowns * (step + 1 - face_x) + unknowns * (1 - face_y)
        width = 5 * unknowns
        for i in range(source // 128, (source + width - 1) // 128 + 1):
            turned = piece[:, 128 * i : 128 * (i + 1)]
            turn = (target - source) % 128
            if turn:
                turned = pltpu.roll(turned, turn, 1)
            first = max(source, 128 * i) - source + target
            last = min(source + width, 128 * (i + 1)) - source + target
            for j in range(first // 128, (last - 1) // 128 + 1):
                low, high = max(first - 128 * j, 0), min(last - 128 * j, 128)
                part = jnp.where((lane >= low) & (lane < high), turned, 0.0)
                tiles[j] = part if tiles[j] is None else tiles[j] + part
    zero = jnp.zeros((piece.shape[0], 128), jnp.float32)
    return [zero if tile is None else tile for tile in tiles]


def one_hot(wanted, source):
    return jnp.where(wanted == source, 1.0, 0.0).astype(jnp.bfloat16)


def pack(block, slots, unknowns):
    span, used = block.shape[0], slots * unknowns
    lane = lax.broadcasted_iota(jnp.int32, (span, 128), 1)
    rest = block[:, 128:].astype(jnp.float32)
    turned = pltpu.roll(rest, 64, 1)
    zero = jnp.zeros_like(rest)
    parts = [jnp.where(lane < 64, rest, zero), jnp.where(lane < 64, zero, turned), jnp.where(lane < 64, turned, rest)]
    stacked = jnp.concatenate([block[:, :128]] + [part.astype(jnp.bfloat16) for part in parts], axis=0)
    row = lax.broadcasted_iota(jnp.int32, (PACK, 4 * span), 0)
    source = lax.broadcasted_iota(jnp.int32, (PACK, 4 * span), 1)
    part, at = source // span, source % span
    dense = at // SLOT * unknowns + at % SLOT
    dense = jnp.where(at % SLOT < unknowns, dense, -1)
    half = used // 2
    low = jnp.where((dense >= 0) & (dense < half), used + dense, -1)
    high = jnp.where(dense >= half, used + dense - half, -1)
    mark = jnp.where(at % SLOT == 0, used + half + at // SLOT, -1)
    goes = jnp.where(part == 0, dense, jnp.where(part == 1, low, jnp.where(part == 2, high, mark)))
    return jnp.dot(one_hot(goes, row), stacked, preferred_element_type=jnp.float32).astype(jnp.bfloat16)


def unpack(packed, slots, unknowns):
    span, used = slots * SLOT, slots * unknowns
    row = lax.broadcasted_iota(jnp.int32, (3 * span, PACK), 0)
    source = lax.broadcasted_iota(jnp.int32, (3 * span, PACK), 1)
    part, at = row // span, row % span
    dense = at // SLOT * unknowns + at % SLOT
    half = used // 2
    folded = used + jnp.where(dense < half, dense, dense - half)
    comes = jnp.where(part == 0, dense, jnp.where(part == 1, folded, used + half + at // SLOT))
    comes = jnp.where((at % SLOT < unknowns) | (part == 2), comes, -1)
    laid = jnp.dot(one_hot(comes, source), packed, preferred_element_type=jnp.float32)
    lane = lax.broadcasted_iota(jnp.int32, (span, 128), 1)
    at = lax.broadcasted_iota(jnp.int32, (span, 128), 0)
    rest = laid[span : 2 * span]
    rest = jnp.where(at // SLOT * unknowns + at % SLOT < half, rest, pltpu.roll(rest, 64, 1))
    rest = jnp.where(lane < 64, rest, laid[2 * span :] + (at % SLOT).astype(jnp.float32))
    return laid[:span].astype(jnp.bfloat16), rest.astype(jnp.bfloat16)


def kernel(
    a_ref, a_codes, p_ref, p_codes, out_ref,
    a_buf, p_buf, mid, inner_side, outer_side, packed, got, half, half_sent, half_got, rows_w, own, send_y, got_y, send_x, got_x,
    a_sem, p_sem, side_out, side_in, mid_out, mid_in, y_out, y_in, x_out, x_in, half_out, half_in, ready,
):
    tile_x, tile_y, slots_a, edges, _ = a_ref.shape
    slots_p, unknowns = p_ref.shape[1], p_ref.shape[2]
    span = slots_p * SLOT
    at_x, at_y = lax.axis_index("gx"), lax.axis_index("gy")
    count_x, count_y = lax.axis_size("gx"), lax.axis_size("gy")
    outer = at_y % 2
    inner = 1 - outer
    rows = (inner, outer)
    sides = (inner_side, outer_side)

    def inside(step_x, step_y):
        there_x, there_y = at_x + step_x, at_y + step_y
        return (there_x >= 0) & (there_x < count_x) & (there_y >= 0) & (there_y < count_y)

    p_copy = pltpu.make_async_copy(p_ref, p_buf, p_sem)
    p_copy.start()
    def start_order(x, y):
        z = y // 2 % 4 * 4 + x // 4
        return (jnp.where(z < 8, 2 * z, jnp.where(z < 12, 16, 15)) + x % 4 + y // 8) * 1024 + x * 32 + y

    def later(step_x, step_y):
        return start_order(at_x + step_x, at_y + step_y) > start_order(at_x, at_y)

    barrier = pltpu.get_barrier_semaphore()
    earlier_ones = jnp.int32(0)
    for step_x, step_y in WAYS:
        there = inside(step_x, step_y)
        comes_later = later(step_x, step_y)
        earlier_ones += (there & jnp.logical_not(comes_later)).astype(jnp.int32)

        @pl.when(there & comes_later)
        def _():
            pl.semaphore_signal(
                barrier, inc=1, device_id=(at_x + step_x, at_y + step_y), device_id_type=pl.DeviceIdType.MESH
            )

    def a_copy(x, y):
        return pltpu.make_async_copy(a_ref.at[x, y], a_buf.at[x, y], a_sem.at[x, y])

    for y in (outer, inner):
        for x in range(tile_x):
            a_copy(x, y).start()

    for way in range(2):
        @pl.when(jnp.logical_not(inside(1 - 2 * way, 0)))
        def _():
            column = (tile_x + 1) * (1 - way)
            mid[:, column] = jnp.zeros((tile_y, span, WIDE), jnp.bfloat16)
            got_x[way] = jnp.zeros(got_x.shape[1:], got_x.dtype)

    for side in range(2):
        step_y = 2 * rows[side] - 1
        for step_x in (-1, 0, 1):
            @pl.when(jnp.logical_not(inside(step_x, step_y)))
            def _():
                columns = {0: slice(1, tile_x + 1), -1: slice(0, 1), 1: slice(tile_x + 1, tile_x + 2)}[step_x]
                holds = got if side else inner_side
                holds[columns] = jnp.zeros_like(holds[columns])
                if step_x == 0:
                    got_y[side] = jnp.zeros(got_y.shape[1:], got_y.dtype)
                    if side:
                        half_got[...] = jnp.zeros_like(half_got)

    rows_w[:, :, :, :, edges:] = jnp.zeros((tile_x, tile_y, slots_a, 2 * span, WIDE - edges), jnp.bfloat16)

    def greet():
        pl.when(earlier_ones > 0)(lambda: pl.semaphore_wait(barrier, earlier_ones))
        for step_x, step_y in WAYS:
            @pl.when(inside(step_x, step_y) & jnp.logical_not(later(step_x, step_y)))
            def _():
                pl.semaphore_signal(
                    ready.at[(1 - step_x) * 3 + 1 - step_y],
                    inc=1,
                    device_id=(at_x + step_x, at_y + step_y),
                    device_id_type=pl.DeviceIdType.MESH,
                )

    def lay_out():
        p_copy.wait()
        taken = slots_p * unknowns * tile_y
        target_row = lax.broadcasted_iota(jnp.int32, (tile_y * span, taken), 0)
        source_row = lax.broadcasted_iota(jnp.int32, (tile_y * span, taken), 1)
        row = lax.broadcasted_iota(jnp.int32, (span, WIDE - edges), 0)
        for x in range(tile_x):
            wanted = jnp.full_like(target_row, -1)
            for y in range(tile_y):
                place = row % SLOT
                for m in range(slots_p):
                    code = p_codes[m, y, x]
                    first_row = y * span + m * SLOT
                    fits = (target_row >= first_row) & (target_row < first_row + unknowns) & (code < 5)
                    wanted = jnp.where(fits, (target_row - first_row + m * unknowns) * tile_y + y, wanted)
                    shift = jnp.where(code == 1, -5, jnp.where(code == 2, 5, jnp.where(code == 3, -1, jnp.where(code == 4, 1, 0))))
                    place = place + jnp.where(row // SLOT == m, shift * unknowns, 0)
                mid[y, x + 1, :, edges:] = place.astype(jnp.float32).astype(jnp.bfloat16)
            order = jnp.where(wanted == source_row, 1.0, 0.0).astype(jnp.bfloat16)
            laid = jnp.dot(order, p_buf[x].reshape(taken, edges), preferred_element_type=jnp.float32).astype(jnp.bfloat16)
            for y in range(tile_y):
                mid[y, x + 1, :, :edges] = laid[y * span : (y + 1) * span]

    steps = start_order(at_x, at_y) // 1024 - start_order(at_x, at_y + 2 * outer - 1) // 1024
    turn = jnp.where((steps >= 0) & (steps <= 3), 1, 0)

    def start_up(i, _):
        pl.when(i == turn)(greet)
        pl.when(i != turn)(lay_out)
        return 0

    lax.fori_loop(0, 2, start_up, 0)

    def side_copy(step_x, side):
        source = {0: pl.ds(1, tile_x), -1: pl.ds(1, 1), 1: pl.ds(tile_x, 1)}[step_x]
        target = {0: pl.ds(1, tile_x), -1: pl.ds(tile_x + 1, 1), 1: pl.ds(0, 1)}[step_x]
        return pltpu.make_async_remote_copy(
            src_ref=packed.at[pl.ds(source.start - 1, source.size)] if side else mid.at[inner, source],
            dst_ref=(got if side else inner_side).at[target],
            send_sem=side_out.at[side, step_x + 1],
            recv_sem=side_in.at[side, step_x + 1],
            device_id=(at_x + step_x, at_y + 2 * rows[side] - 1),
            device_id_type=pl.DeviceIdType.MESH,
        )

    def mid_copy(way):
        return pltpu.make_async_remote_copy(
            src_ref=mid.at[:, pl.ds(1 + (tile_x - 1) * way, 1)],
            dst_ref=mid.at[:, pl.ds((tile_x + 1) * (1 - way), 1)],
            send_sem=mid_out.at[way],
            recv_sem=mid_in.at[way],
            device_id=(at_x + 2 * way - 1, at_y),
            device_id_type=pl.DeviceIdType.MESH,
        )

    def y_copy(side):
        return pltpu.make_async_remote_copy(
            src_ref=send_y.at[side],
            dst_ref=got_y.at[side],
            send_sem=y_out.at[side],
            recv_sem=y_in.at[side],
            device_id=(at_x, at_y + 2 * rows[side] - 1),
            device_id_type=pl.DeviceIdType.MESH,
        )

    def x_copy(way, side):
        return pltpu.make_async_remote_copy(
            src_ref=send_x.at[way, side],
            dst_ref=got_x.at[way, side],
            send_sem=x_out.at[way, side],
            recv_sem=x_in.at[way, side],
            device_id=(at_x + 2 * way - 1, at_y),
            device_id_type=pl.DeviceIdType.MESH,
        )

    def half_copy():
        return pltpu.make_async_remote_copy(
            src_ref=half_sent,
            dst_ref=half_got,
            send_sem=half_out,
            recv_sem=half_in,
            device_id=(at_x, at_y + 2 * outer - 1),
            device_id_type=pl.DeviceIdType.MESH,
        )

    def when_inside(step_x, step_y, does):
        pl.when(inside(step_x, step_y))(does)

    def outward_slot(x, i):
        slot, found = jnp.int32(0), False
        for k in range(slots_a):
            fits = a_codes[x, outer, k] == 3 * i + 2 * outer
            slot, found = jnp.where(fits, k, slot), found | fits
        return slot, found

    def first(side):
        y = rows[side]
        for x in range(tile_x):
            a_copy(x, y).wait()
            here = mid[y, x + 1, :, :edges]
            for k in range(slots_a):
                product = jnp.dot(here, a_buf[x, y, k], preferred_element_type=jnp.float32)
                high = product.astype(jnp.bfloat16)
                low = (product - high.astype(jnp.float32)).astype(jnp.bfloat16)
                rows_w[x, y, k, :span, :edges] = high
                rows_w[x, y, k, span:, :edges] = low
            if side:
                for i in range(3):
                    slot, found = outward_slot(x, i)
                    leaves = jnp.zeros((SLOT, WIDE), jnp.bfloat16)
                    for m in range(1, slots_p):
                        block = rows_w[x, y, slot, SLOT * m : SLOT * (m + 1)]
                        leaves = jnp.where(found & (p_codes[m, y, x] == y + 3), block, leaves)
                    half[x, SLOT * i : SLOT * (i + 1)] = leaves
                half_sent[x] = pack(half[x], slots_p, unknowns)

    lane = lax.broadcasted_iota(jnp.int32, (span, COLS), 1).astype(jnp.float32)

    def placed(block, there, base):
        target = there[:, edges : edges + 1].astype(jnp.float32) + base
        chosen = jnp.where(lane == target, 1.0, 0.0).astype(jnp.bfloat16)
        return jnp.dot(block.astype(jnp.bfloat16), chosen, preferred_element_type=jnp.float32)

    def across(left, there):
        return lax.dot_general(left, there, (((1,), (1,)), ((), ())), preferred_element_type=jnp.float32)

    def store(x, y, summed, add):
        def put_own(q, value):
            own[q, x, y] = own[q, x, y] + value if add else value

        put_own(0, summed[:SLOT])
        for q in range(1, 5):
            value = jnp.zeros((SLOT, COLS), jnp.float32)
            for m in range(1, slots_p):
                value += jnp.where(p_codes[m, y, x] == q, summed[SLOT * m : SLOT * (m + 1)], 0.0)
            put_own(q, value)

    def second(side):
        y = rows[side]
        for x in range(tile_x):
            summed = jnp.zeros((span, COLS), jnp.float32)
            for k in range(slots_a):
                code = a_codes[x, y, k]
                live = code < 9
                code = jnp.where(live, code, 4)
                step_x, step_y = code // 3 - 1, code % 3 - 1
                away = step_y == 2 * y - 1
                there = mid[jnp.clip(y + step_y, 0, tile_y - 1), x + 1 + step_x]
                if side:
                    live = live & jnp.logical_not(away)
                else:
                    there = jnp.where(away, inner_side[x + 1 + step_x], there)
                base = jnp.where(live, unknowns * (5 * (step_x + 2) + step_y + 2), -4096).astype(jnp.float32)
                both = across(rows_w[x, y, k], there)
                summed += placed(both[:span] + both[span:], there, base)
            store(x, y, summed, False)

    def second_outward():
        for x in range(tile_x):
            summed = jnp.zeros((span, COLS), jnp.float32)
            for i in range(3):
                there = outer_side[x + i]
                slot, found = outward_slot(x, i)
                base = jnp.where(found, unknowns * (5 * (i + 1) + 2 * outer + 1), -4096).astype(jnp.float32)
                both = across(rows_w[x, outer, slot], there)
                summed += placed(both[:span] + both[span:], there, base)
            store(x, outer, summed, True)

    def second_inward(x):
        high, rest = unpack(half_got[x], slots_p, unknowns)
        rest = jnp.where(lax.broadcasted_iota(jnp.int32, rest.shape, 1) < edges - 128, rest, jnp.zeros_like(rest))
        left = jnp.concatenate([high, rest], axis=1)
        summed = jnp.zeros((SLOT, COLS), jnp.float32)
        for i in range(3):
            there = mid[outer, x + i]
            product = across(left[SLOT * i : SLOT * (i + 1)], there)
            summed += placed(product, there, float(unknowns * (5 * (i + 1) + 2)))
        return summed

    def send_y_contributions(side):
        y = rows[side]
        for x in range(tile_x):
            send_y[side, x] = own[y + 3, x, y].astype(jnp.bfloat16)
        when_inside(0, 2 * y - 1, lambda: y_copy(side).start())

    def send_x_contributions(side):
        y = rows[side]
        for way in range(2):
            send_x[way, side] = own[way + 1, (tile_x - 1) * way, y].astype(jnp.bfloat16)
            when_inside(2 * way - 1, 0, lambda: x_copy(way, side).start())

    for x in range(tile_x):
        packed[x] = pack(mid[outer, x + 1], slots_p, unknowns)

    outer_copies = [(step_x, 2 * outer - 1, functools.partial(side_copy, step_x, 1)) for step_x in (0, -1, 1)]
    inner_copies = [(step_x, 2 * inner - 1, functools.partial(side_copy, step_x, 0)) for step_x in (0, -1, 1)]
    mid_copies = [(2 * way - 1, 0, functools.partial(mid_copy, way)) for way in range(2)]
    for step_x, step_y, copy in outer_copies + mid_copies + inner_copies:
        pl.when(inside(step_x, step_y) & jnp.logical_not(later(step_x, step_y)))(lambda: copy().start())
    for step_x, step_y, copy in mid_copies + inner_copies + outer_copies:
        @pl.when(inside(step_x, step_y) & later(step_x, step_y))
        def _():
            pl.semaphore_wait(ready.at[(step_x + 1) * 3 + step_y + 1], 1)
            copy().start()

    first(1)
    when_inside(0, 2 * outer - 1, lambda: half_copy().start())
    for way in range(2):
        when_inside(1 - 2 * way, 0, lambda: mid_copy(way).wait_recv())
    second(1)
    send_y_contributions(1)

    first(0)
    for step_x in (0, -1, 1):
        when_inside(-step_x, 2 * inner - 1, lambda: side_copy(step_x, 0).wait_recv())
    second(0)
    send_y_contributions(0)
    send_x_contributions(0)

    def put(x, y, pieces, add):
        total = None
        for piece, face in pieces:
            tiles = spread_out(piece.astype(jnp.float32), FACES[face], unknowns)
            total = tiles if total is None else [s + t for s, t in zip(total, tiles)]
        for j, tile in enumerate(total):
            high = min(128 * (j + 1), out_ref.shape[3])
            tile = tile[:unknowns, : high - 128 * j]
            if add:
                tile = tile + out_ref[x, y, :, 128 * j : high]
            out_ref[x, y, :, 128 * j : high] = tile

    for step_x in (0, -1, 1):
        when_inside(-step_x, 2 * outer - 1, lambda: side_copy(step_x, 1).wait_recv())
    for x in range(tile_x + 2):
        outer_side[x, :, :128], outer_side[x, :, 128:] = unpack(got[x], slots_p, unknowns)
    second_outward()
    send_x_contributions(1)

    for x in range(tile_x):
        for y in range(tile_y):
            pieces = []
            for face, (face_x, face_y) in enumerate(FACES):
                from_x, from_y = x - face_x, y - face_y
                if 0 <= from_x < tile_x and 0 <= from_y < tile_y:
                    pieces.append((own[face, from_x, from_y], face))
            put(x, y, pieces, False)

    when_inside(0, 2 * outer - 1, lambda: half_copy().wait_recv())
    for x in range(tile_x):
        put(x, outer, [(second_inward(x), 0)], True)

    for way in range(2):
        for side in range(2):
            when_inside(1 - 2 * way, 0, lambda: x_copy(way, side).wait_recv())
    for side in range(2):
        when_inside(0, 2 * rows[side] - 1, lambda: y_copy(side).wait_recv())

    for x in range(tile_x):
        for y in range(tile_y):
            side = outer if y else inner
            pieces = [(got_y[side, x], 4 - y)]
            if x == 0:
                pieces.append((got_x[1, side], 2))
            if x == tile_x - 1:
                pieces.append((got_x[0, side], 1))
            put(x, y, pieces, True)

    for side in range(2):
        for step_x in (-1, 0, 1):
            when_inside(step_x, 2 * rows[side] - 1, lambda: side_copy(step_x, side).wait_send())
        when_inside(0, 2 * rows[side] - 1, lambda: y_copy(side).wait_send())
        for way in range(2):
            when_inside(2 * way - 1, 0, lambda: x_copy(way, side).wait_send())
    for way in range(2):
        when_inside(2 * way - 1, 0, lambda: mid_copy(way).wait_send())
    when_inside(0, 2 * outer - 1, lambda: half_copy().wait_send())


def shards(a_blocks, a_codes, p_blocks, p_codes):
    tile_x, tile_y, slots_a = a_codes.shape
    slots_p, unknowns, edges = p_blocks.shape[2:]
    span = slots_p * SLOT
    dma = pltpu.SemaphoreType.DMA
    return pl.pallas_call(
        kernel,
        out_shape=jax.ShapeDtypeStruct((tile_x, tile_y, unknowns, 49 * unknowns), jnp.float32),
        in_specs=[
            pl.BlockSpec(memory_space=pltpu.HBM),
            pl.BlockSpec(memory_space=pltpu.SMEM),
            pl.BlockSpec(memory_space=pltpu.HBM),
            pl.BlockSpec(memory_space=pltpu.SMEM),
        ],
        out_specs=pl.BlockSpec(memory_space=pltpu.VMEM),
        scratch_shapes=[
            pltpu.VMEM((tile_x, tile_y, slots_a, edges, edges), jnp.bfloat16),
            pltpu.VMEM((tile_x, slots_p, unknowns, tile_y, edges), jnp.bfloat16),
            pltpu.VMEM((tile_y, tile_x + 2, span, WIDE), jnp.bfloat16),
            pltpu.VMEM((tile_x + 2, span, WIDE), jnp.bfloat16),
            pltpu.VMEM((tile_x + 2, span, WIDE), jnp.bfloat16),
            pltpu.VMEM((tile_x, PACK, 128), jnp.bfloat16),
            pltpu.VMEM((tile_x + 2, PACK, 128), jnp.bfloat16),
            pltpu.VMEM((tile_x, span, WIDE), jnp.bfloat16),
            pltpu.VMEM((tile_x, PACK, 128), jnp.bfloat16),
            pltpu.VMEM((tile_x, PACK, 128), jnp.bfloat16),
            pltpu.VMEM((tile_x, tile_y, slots_a, 2 * span, WIDE), jnp.bfloat16),
            pltpu.VMEM((5, tile_x, tile_y, SLOT, COLS), jnp.float32),
            pltpu.VMEM((tile_y, tile_x, SLOT, COLS), jnp.bfloat16),
            pltpu.VMEM((tile_y, tile_x, SLOT, COLS), jnp.bfloat16),
            pltpu.VMEM((2, tile_y, SLOT, COLS), jnp.bfloat16),
            pltpu.VMEM((2, tile_y, SLOT, COLS), jnp.bfloat16),
            dma((tile_x, tile_y)),
            dma,
            dma((2, 3)),
            dma((2, 3)),
            dma((2,)),
            dma((2,)),
            dma((2,)),
            dma((2,)),
            dma((2, 2)),
            dma((2, 2)),
            dma,
            dma,
            pltpu.SemaphoreType.REGULAR((9,)),
        ],
        compiler_params=pltpu.CompilerParams(
            collective_id=0, has_side_effects=True, vmem_limit_bytes=40 * 2**20
        ),
    )(pltpu.with_memory_space_constraint(a_blocks, pltpu.HBM), pltpu.with_memory_space_constraint(a_codes, pltpu.HBM), pltpu.with_memory_space_constraint(jnp.transpose(p_blocks, (0, 2, 3, 1, 4)), pltpu.HBM), pltpu.with_memory_space_constraint(jnp.transpose(p_codes, (2, 1, 0)), pltpu.HBM))


def solution(mesh):
    in_specs = (
        P("gx", "gy", None, None, None),
        P("gx", "gy", None),
        P("gx", "gy", None, None, None),
        P("gx", "gy", None),
    )
    out_specs = P("gx", "gy", None, None)
    return jax.shard_map(shards, mesh=mesh, in_specs=in_specs, out_specs=out_specs, check_vma=False)
```
